128 devices in a mesh: view: 16 (over x, y), edge: 8 (over z, core).
Axes of the slice: x: 4, y: 4, z: 4, core: 2. Of those that a mesh axis runs over, the one named last changes fastest.
Arguments:
- log_depth: float32 [1024, 12288], P('view', 'edge'), may hold values from -0.6 to 0.6
- depth_m: float32 [1024, 12288], P('view', 'edge'), may hold values from -12 to 12
- depth_v: float32 [1024, 12288], P('view', 'edge'), may hold values from 1 to 100
- pose: float32 [13, 1024], P(None, ('view', 'edge')), may hold values from -1 to 6, as said below
- pose_m: float32 [13, 1024], P(None, ('view', 'edge')), may hold values from -5 to 5
- pose_v: float32 [13, 1024], P(None, ('view', 'edge')), may hold values from 0.1 to 10
- pairs: int32 [2048, 2], replicated, may hold values from 0 to 1023, as said below
- points: bfloat16 [2048, 3, 12288], P(('view', 'edge')), may hold values from -6 to 6
- conf: bfloat16 [2048, 12288], P(('view', 'edge')), may hold values from 1 to 10
Outputs:
- new_depth: float32 [1024, 12288], P('view', 'edge')
- new_depth_m: float32 [1024, 12288], P('view', 'edge')
- new_depth_v: float32 [1024, 12288], P('view', 'edge')
- new_pose: float32 [13, 1024], P(None, ('view', 'edge'))
- new_pose_m: float32 [13, 1024], P(None, ('view', 'edge'))
- new_pose_v: float32 [13, 1024], P(None, ('view', 'edge'))
The draws below stay inside these ranges and needn't reach their ends.
Inputs may be any that keep to these rules, and one draw needn't show every extreme that they name: `pairs`: row e is edge e; rows d * 16 to (d + 1) * 16 - 1 are the edges of device d of view+edge. Column 0 is the view whose camera frame the pointmap is given in, column 1 the view whose pixels it covers. Among one device's edges at most 2 name a second view in any one block of 64 consecutive views, and exactly 2 do so in at least one block. `pose`: rows 0-8 hold each view's matrix near the identity, rows 9-11 its centre, row 12 a log focal length between log 80 and log 160.
All inputs are finite; a program needn't handle non-finite values.
Results may differ from the reference program's by a relative error of at most 0.0017.
Values may be sent and summed in bfloat16 or wider, within the bound.
No kernel may reach another device: no remote copies, remote signals or barrier semaphores. Data moves between devices by JAX's collectives and lax.ppermute only.
A program may use at most 64 MiB of HBM per device.

```python
import math
import jax
import jax.numpy as jnp
from jax import lax

H = 128
W = 96
POSE_ROWS = 13
V_DEV = 64
E_DEV = 16
ITERS = 2
STEPS_DONE = 10
GROUPS = 16
OWNERS = 128
VIEWS = 1024
EDGES = 2048
CAP = 2


def draw_pose(key, part):
    key = jax.random.fold_in(key, 7)
    key_mix = jax.random.fold_in(key, 0)
    key_shift = jax.random.fold_in(key, 2)
    key_focal = jax.random.fold_in(key, 3)
    mix = jax.random.uniform(key_mix, (9, VIEWS), jnp.float32, -0.3, 0.3)
    shift = jax.random.uniform(key_shift, (3, VIEWS), jnp.float32, -0.6, 0.6)
    matrix = jnp.eye(3, dtype=jnp.float32).reshape(9, 1) + mix
    focal = jnp.log(jax.random.uniform(key_focal, (1, VIEWS), jnp.float32, 80.0, 160.0))
    return jnp.concatenate([matrix, shift, focal], axis=0).astype(jnp.float32)


def draw_pairs(key, part):
    key = jax.random.fold_in(key, 11)
    keys = jax.random.split(key, 6)
    slots = (GROUPS - 1) * (CAP - 1)
    leading = jax.random.randint(keys[0], (OWNERS,), 0, GROUPS)
    score = jax.random.randint(keys[1], (OWNERS, slots), 0, 1 << 20) * slots + jnp.arange(slots, dtype=jnp.int32)[None, :]
    chosen = jnp.argsort(score, axis=1)[:, :E_DEV - CAP].astype(jnp.int32)
    later = 1 + chosen // (CAP - 1)
    shifts = jnp.concatenate([jnp.zeros((OWNERS, CAP), jnp.int32), later], axis=1)
    mixing = jax.random.randint(keys[2], (OWNERS, E_DEV), 0, 1 << 20) * E_DEV + jnp.arange(E_DEV, dtype=jnp.int32)[None, :]
    order = jnp.argsort(mixing, axis=1).astype(jnp.int32)
    shifts = jnp.take_along_axis(shifts, order, axis=1)
    group = (leading[:, None] + shifts) % GROUPS
    offset = jnp.minimum(jax.random.randint(keys[3], (OWNERS, E_DEV), 0, V_DEV), jax.random.randint(keys[4], (OWNERS, E_DEV), 0, V_DEV))
    second = group * V_DEV + offset
    first = jax.random.randint(keys[5], (OWNERS, E_DEV), 0, VIEWS)
    return jnp.stack([first.reshape(-1), second.reshape(-1)], axis=1).astype(jnp.int32)


def levels(key, extent, cuts, smallest, top_value):
    loudness = 1.0
    for position, shards_of in cuts:
        draws = jax.random.uniform(jax.random.fold_in(jax.random.fold_in(key, 6), position), (shards_of,), jnp.float32, smallest / len(cuts), top_value / len(cuts))
        loudness = loudness * jnp.repeat(jnp.exp(draws), extent[position] // shards_of).reshape((-1,) + (1,) * (len(extent) - 1 - position))
    return loudness


def gaussian(own_key, dims, deviation, most, cuts=(), kind=jnp.bfloat16):
    entries = jax.random.normal(own_key, dims, jnp.float32) * deviation
    if len(cuts) > 0:
        entries = levels(own_key, dims, cuts, -0.22, 0.18) * entries
    return jnp.clip(entries, min=-most, max=most).astype(kind)


def setup_inputs(seed: int = 0) -> dict:
    arg_keys = jax.random.split(jax.random.key(seed), 10)
    log_depth = jnp.clip(jax.random.uniform(arg_keys[0], (VIEWS, H * W), jnp.float32, -0.6, 0.6) * levels(arg_keys[0], (VIEWS, H * W), ((0, 16), (1, 8)), -0.4, 0.0), -0.6, 0.6)
    depth_m = gaussian(arg_keys[1], (VIEWS, H * W), 3.0, 12.0, ((0, 16), (1, 8)), jnp.float32)
    depth_v = jnp.clip(jnp.exp(math.log(100.0) - 4.6051702 * jax.random.uniform(arg_keys[2], (VIEWS, H * W), jnp.float32) ** levels(arg_keys[2], (VIEWS, H * W), ((0, 16), (1, 8)), -0.2, 0.2)), 1.0, 100.0)
    pose = draw_pose(jax.random.fold_in(arg_keys[9], 71), 0)
    pose_m = gaussian(arg_keys[4], (POSE_ROWS, VIEWS), 1.0, 5.0, ((1, 128),), jnp.float32)
    pose_v = jnp.clip(jnp.exp(math.log(10.0) - 4.6051702 * jax.random.uniform(arg_keys[5], (POSE_ROWS, VIEWS), jnp.float32) ** levels(arg_keys[5], (POSE_ROWS, VIEWS), ((1, 128),), -0.2, 0.2)), 0.1, 10.0)
    pairs = draw_pairs(jax.random.fold_in(arg_keys[9], 71), 0)
    points = gaussian(arg_keys[7], (EDGES, 3, H * W), 1.0, 6.0, ((0, 128),))
    conf = jnp.clip(jnp.exp(math.log(10.0) - 2.3025851 * jax.random.uniform(arg_keys[8], (EDGES, H * W), jnp.float32) ** levels(arg_keys[8], (EDGES, H * W), ((0, 128),), -0.2, 0.2)), 1.0, 10.0).astype(jnp.bfloat16)
    return {"log_depth": log_depth, "depth_m": depth_m, "depth_v": depth_v, "pose": pose, "pose_m": pose_m, "pose_v": pose_v, "pairs": pairs, "points": points, "conf": conf}


learn_rate = 0.01
beta_first = 0.9
beta_second = 0.999
adam_eps = 1e-08

def pixel_rays(map_cells, columns, lines):
    index = jnp.arange(map_cells, dtype=jnp.int32)
    ray_u = (index % columns).astype(jnp.float32) - (columns - 1) / 2.0
    ray_v = (index // columns).astype(jnp.float32) - (lines - 1) / 2.0
    return (ray_u, ray_v)

def edge_loss(depth_log, pose_first, pose_second, points, conf, ray_u, ray_v):
    focal = jnp.exp(pose_second[12])[:, None]
    depth = jnp.exp(depth_log)
    camera = (depth * ray_u[None, :] / focal, depth * ray_v[None, :] / focal, depth)
    offsets = []
    for outer in range(3):
        world = pose_second[9 + outer][:, None] + pose_second[3 * outer][:, None] * camera[0]
        world = world + pose_second[3 * outer + 1][:, None] * camera[1] + pose_second[3 * outer + 2][:, None] * camera[2]
        offsets.append(world - pose_first[9 + outer][:, None])
    squares = jnp.zeros_like(depth)
    for outer in range(3):
        viewed = pose_first[outer][:, None] * offsets[0] + pose_first[3 + outer][:, None] * offsets[1]
        viewed = viewed + pose_first[6 + outer][:, None] * offsets[2]
        mismatch = viewed - points[:, outer, :].astype(jnp.float32)
        squares = squares + mismatch * mismatch
    return jnp.sum(conf.astype(jnp.float32) * squares)

def edge_grads(depth_log, pose_first, pose_second, points, conf, ray_u, ray_v):

    def local_loss(depth_arg, first_arg, second_arg):
        return edge_loss(depth_arg, first_arg, second_arg, points, conf, ray_u, ray_v)
    value, pull = jax.vjp(local_loss, depth_log, pose_first, pose_second)
    return pull(jnp.ones((), jnp.float32))

def adam_update(param, moment, second, grad, count):
    moment = beta_first * moment + (1.0 - beta_first) * grad
    second = beta_second * second + (1.0 - beta_second) * grad * grad
    corrected = moment / (1.0 - beta_first ** count)
    spread = second / (1.0 - beta_second ** count)
    return (param - learn_rate * corrected / (jnp.sqrt(spread) + adam_eps), moment, second)

def reference(log_depth, depth_m, depth_v, pose, pose_m, pose_v, pairs, points, conf):
    map_cells = H * W
    ray_u, ray_v = pixel_rays(map_cells, W, H)
    blocks = EDGES // E_DEV
    first_all = pairs[:, 0].reshape(blocks, E_DEV)
    second_all = pairs[:, 1].reshape(blocks, E_DEV)
    block_points = points.reshape(blocks, E_DEV, 3, map_cells)
    block_conf = conf.reshape(blocks, E_DEV, map_cells)
    for turn in range(ITERS):
        rounded = lax.optimization_barrier(log_depth.astype(jnp.bfloat16)).astype(jnp.float32)

        def block_step(carry, items):
            depth_acc, pose_acc = carry
            first, second, these_points, these_conf = items
            grads = edge_grads(rounded[second], pose[:, first], pose[:, second], these_points, these_conf, ray_u, ray_v)
            depth_acc = depth_acc.at[second].add(grads[0])
            pose_acc = pose_acc.at[:, first].add(grads[1]).at[:, second].add(grads[2])
            return ((depth_acc, pose_acc), None)
        start = (jnp.zeros((VIEWS, map_cells), jnp.float32), jnp.zeros((POSE_ROWS, VIEWS), jnp.float32))
        carry, unused = lax.scan(block_step, start, (first_all, second_all, block_points, block_conf))
        depth_grad = carry[0]
        pose_grad = carry[1] / float(map_cells)
        count = STEPS_DONE + turn + 1
        log_depth, depth_m, depth_v = adam_update(log_depth, depth_m, depth_v, depth_grad, count)
        pose, pose_m, pose_v = adam_update(pose, pose_m, pose_v, pose_grad, count)
    return (log_depth, depth_m, depth_v, pose, pose_m, pose_v)
```

```python
import functools

import jax
import jax.numpy as jnp
from jax import lax
from jax.experimental import pallas as pl
from jax.experimental.pallas import tpu as pltpu
from jax.sharding import PartitionSpec as P

H = 128
W = 96
ITERS = 2
STEPS_DONE = 10
ROWS = 13
LANES = 128
CAP = 2

learn_rate = 0.01
beta_first = 0.9
beta_second = 0.999
adam_eps = 1e-08

f32 = jnp.float32
bf16 = jnp.bfloat16
EXACT = lax.Precision.HIGHEST


def adam(param, moment, second, grad, count):
    moment = beta_first * moment + (1.0 - beta_first) * grad
    second = beta_second * second + (1.0 - beta_second) * grad * grad
    corrected = moment * (learn_rate / (1.0 - beta_first**count))
    spread = second * (1.0 / (1.0 - beta_second**count))
    return (param - corrected / (jnp.sqrt(spread) + adam_eps), moment, second)


def iota(shape, dim):
    return lax.broadcasted_iota(jnp.int32, shape, dim)


def dot(a, b, dims=((1,), (0,)), precision=None):
    return lax.dot_general(a, b, (dims, ((), ())), precision=precision, preferred_element_type=f32)


def fold_matrix():
    return (iota((LANES, LANES), 0) // 8 == iota((LANES, LANES), 1)).astype(f32)


def hot(mask):
    return jnp.where(mask, 1.0, 0.0).astype(bf16)


def make_picker(local):
    rows, edges = local.shape
    hit = (local >= 0) & (local < 64)
    tri = hot(iota((edges, edges), 0) < iota((edges, edges), 1))
    rank = dot(hot(hit), tri)
    slot = (iota((rows, edges), 0) % CAP).astype(f32)
    mine = hit & (rank == slot)
    target = jnp.sum(jnp.where(mine, local + 1, 0).astype(f32), axis=1, keepdims=True)
    return hot((iota((rows, 64), 1) + 1).astype(f32) == target)


def spread_pose(pose_t):
    wide = dot(pose_t, fold_matrix()[:, :ROWS], ((1,), (1,)), EXACT)
    mine = iota(wide.shape, 1) % 8 == iota(wide.shape, 0)
    return jnp.sum(jnp.where(mine, wide, 0.0), axis=0, keepdims=True)


def gather_pose(row):
    wide = jnp.broadcast_to(row, (8, LANES))
    mine = iota(wide.shape, 1) % 8 == iota(wide.shape, 0)
    return dot(jnp.where(mine, wide, 0.0), fold_matrix()[:, :ROWS], ((1,), (0,)), EXACT)


def two_parts(rows):
    lead = rows.astype(bf16).astype(f32)
    even = iota(rows.shape, 0) % 2 == 0
    return jnp.where(even, lead, rows - lead).astype(bf16)


def send_rows(out, picker, depth, pose_row):
    owners, cap, width = out.shape
    pixels = width - LANES
    picked = dot(picker, depth.astype(bf16)).astype(bf16)
    out[:, :, :pixels] = picked.reshape(owners, cap, pixels)
    wide = jnp.broadcast_to(pose_row, (owners * cap, LANES))
    out[:, :, pixels:] = two_parts(wide).reshape(owners, cap, LANES)


def first_kernel(local, depth, pose_t, out, picker_out):
    picker = make_picker(local[...])
    picker_out[...] = picker
    send_rows(out, picker, depth[...], spread_pose(pose_t[...]))


def owner_kernel(count, last, incoming, picker, depth, m, v, pose_t, pose_m, pose_v, *outs):
    owners, cap, width = incoming.shape
    pixels = width - LANES
    grad = dot(picker[...], incoming[:, :, :pixels].reshape(owners * cap, pixels), ((0,), (0,)))
    new = adam(depth[...], m[...], v[...], grad, count)
    for ref, value in zip(outs[:3], new):
        ref[...] = value
    rows = incoming[:, :, pixels:].reshape(owners * cap, LANES)
    pose_grad = jnp.sum(rows.astype(f32), axis=0, keepdims=True) * (1.0 / (pixels * 8))
    state = [spread_pose(ref[...]) for ref in (pose_t, pose_m, pose_v)]
    new_pose = adam(*state, pose_grad, count)
    for ref, value in zip(outs[3:6], new_pose):
        ref[...] = gather_pose(value)
    if not last:
        send_rows(outs[6], picker[...], new[0], new_pose[0])


def edge_kernel(arrived, mine, mine_t, points, conf, out, depth_s, grad_s):
    groups, shards, cap, width = arrived.shape
    pixels = width - LANES
    edges = mine.shape[0]
    owners = groups * shards
    group = mine[:, 1:2] // 64
    group_row = mine_t[1:2, :] // 64
    earlier = iota((edges, edges), 1) < iota((edges, edges), 0)
    slot = jnp.sum(jnp.where((group == group_row) & earlier, 1.0, 0.0), axis=1, keepdims=True)
    sel = hot((group * cap).astype(f32) + slot == iota((edges, groups * cap), 1).astype(f32))

    for s in range(shards):
        rows = arrived[:, s, :, :pixels].reshape(groups * cap, pixels)
        depth_s[:, s * pixels : (s + 1) * pixels] = dot(sel, rows)

    both = jnp.concatenate([mine[:, 0:1], mine[:, 1:2]], axis=0)
    pose_rows = arrived[:, :, :, pixels:].reshape(owners * cap, LANES)
    owner_hot = hot(iota((2 * edges, owners * cap), 1) // cap == both // 8)
    lane_mask = iota((2 * edges, LANES), 1) % 8 == both % 8
    fold = fold_matrix()
    wide = jnp.where(lane_mask, dot(owner_hot, pose_rows), 0.0)
    poses = dot(wide, fold, ((1,), (0,)), EXACT)
    pf = [poses[:edges, k : k + 1] for k in range(12)]
    ps = [poses[edges:, k : k + 1] for k in range(13)]
    inv_f = jnp.exp(-ps[12])
    shift = [ps[9 + b] - pf[9 + b] for b in range(3)]
    mix = [[sum(pf[3 * b + a] * ps[3 * b + c] for b in range(3)) for c in range(3)] for a in range(3)]
    base = [sum(pf[3 * b + a] * shift[b] for b in range(3)) for a in range(3)]
    alpha = [mix[a][0] * inv_f for a in range(3)]
    beta = [mix[a][1] * inv_f for a in range(3)]
    tile = (edges, LANES)
    wide_alpha = [jnp.broadcast_to(x, tile) for x in alpha]
    wide_beta = [jnp.broadcast_to(x, tile) for x in beta]
    wide_gamma = [jnp.broadcast_to(mix[a][2], tile) for a in range(3)]
    wide_base = [jnp.broadcast_to(x, tile) for x in base]

    period = 3 * LANES
    lines = period // W
    lane = iota((1, LANES), 1)
    us = []
    vs = []
    for k in range(3):
        index = lane + k * LANES
        line = sum((index >= W * (j + 1)).astype(jnp.int32) for j in range(lines - 1))
        us.append((index - line * W).astype(f32) - (W - 1) / 2.0)
        vs.append(line.astype(f32) - (H - 1) / 2.0)

    def step(i, sums):
        sums = list(sums)
        for k in range(3):
            at = pl.ds(pl.multiple_of(i * period + k * LANES, LANES), LANES)
            u = us[k]
            v = vs[k] + (i * lines).astype(f32)
            dep = jnp.exp(depth_s[:, at])
            weight = conf[:, at].astype(f32)
            weight = weight + weight
            grad = None
            for a in range(3):
                q = wide_alpha[a] * u + (wide_beta[a] * v + wide_gamma[a])
                r = weight * (dep * q + (wide_base[a] - points[a, :, at].astype(f32)))
                t = r * dep
                grad = t * q if grad is None else grad + t * q
                sums[a] = sums[a] + r
                sums[3 + a] = sums[3 + a] + t * u
                sums[6 + a] = sums[6 + a] + t * v
                sums[9 + a] = sums[9 + a] + t
            grad_s[:, at] = grad.astype(bf16)
        return tuple(sums)

    zero = jnp.zeros(tile, f32)
    sums = lax.fori_loop(0, shards * pixels // period, step, (zero,) * 12)
    sums = [jnp.sum(x, axis=1, keepdims=True) for x in sums]

    for s in range(shards):
        placed = dot(sel, grad_s[:, s * pixels : (s + 1) * pixels], ((0,), (0,))).astype(bf16)
        out[:, s, :, :pixels] = placed.reshape(groups, cap, pixels)

    s_sum, u_sum, v_sum, d_sum = sums[:3], sums[3:6], sums[6:9], sums[9:]
    moments = [[u_sum[a] * inv_f, v_sum[a] * inv_f, d_sum[a]] for a in range(3)]
    grad_first = [None] * 13
    grad_second = [None] * 13
    for b in range(3):
        for a in range(3):
            grad_first[3 * b + a] = sum(ps[3 * b + c] * moments[a][c] for c in range(3)) + shift[b] * s_sum[a]
        for c in range(3):
            grad_second[3 * b + c] = sum(pf[3 * b + a] * moments[a][c] for a in range(3))
        grad_second[9 + b] = sum(pf[3 * b + a] * s_sum[a] for a in range(3))
        grad_first[9 + b] = -grad_second[9 + b]
    grad_second[12] = -sum(alpha[a] * u_sum[a] + beta[a] * v_sum[a] for a in range(3))
    lanes = iota(tile, 1)
    tables = []
    for grads in (grad_first, grad_second):
        table = jnp.zeros(tile, f32)
        for k, g in enumerate(grads):
            if g is not None:
                table = jnp.where(lanes == k, g, table)
        tables.append(table)
    table = jnp.concatenate(tables, axis=0)
    expanded = jnp.where(lane_mask, dot(table, fold, ((1,), (1,)), EXACT), 0.0)
    owned = dot(owner_hot.astype(f32), expanded, ((0,), (0,)), EXACT)
    out[:, :, :, pixels:] = two_parts(owned).reshape(groups, shards, cap, LANES)


def call(kernel, outs, scratch=()):
    return pl.pallas_call(
        kernel,
        out_shape=outs,
        scratch_shapes=list(scratch),
        compiler_params=pltpu.CompilerParams(vmem_limit_bytes=40 * 1024 * 1024),
    )


def shards(log_depth, depth_m, depth_v, pose, pose_m, pose_v, pairs, points, conf):
    n_view = lax.axis_size("view")
    n_edge = lax.axis_size("edge")
    owners = n_view * n_edge
    views, pixels = log_depth.shape
    edges = points.shape[0]
    width = pixels + LANES
    me = lax.axis_index(("view", "edge"))
    seconds = pairs[:, 1].reshape(owners, edges)
    local = jnp.repeat(seconds - lax.axis_index("view") * views, CAP, axis=0)
    mine = lax.dynamic_slice_in_dim(pairs, me * edges, edges, 0)
    planes = points.transpose(1, 0, 2)

    S = jax.ShapeDtypeStruct
    message = S((owners, CAP, width), bf16)
    depth_out = [S((views, pixels), f32)] * 3
    pose_out = [S((8, ROWS), f32)] * 3
    exchange = functools.partial(
        lax.all_to_all, axis_name=("view", "edge"), split_axis=0, concat_axis=0, tiled=True
    )

    poses = [pose.T, pose_m.T, pose_v.T]
    depths = [log_depth, depth_m, depth_v]
    sending, picker = call(first_kernel, [message, S((owners * CAP, views), bf16)])(
        local, log_depth, poses[0]
    )
    for turn in range(ITERS):
        arrived = exchange(sending).reshape(n_view, n_edge, CAP, width)
        back = call(
            edge_kernel,
            S((n_view, n_edge, CAP, width), bf16),
            [pltpu.VMEM((edges, pixels * n_edge), f32), pltpu.VMEM((edges, pixels * n_edge), bf16)],
        )(arrived, mine, mine.T, planes, conf)
        incoming = exchange(back.reshape(owners, CAP, width))
        last = turn == ITERS - 1
        kernel = functools.partial(owner_kernel, STEPS_DONE + turn + 1, last)
        results = call(kernel, depth_out + pose_out + ([] if last else [message]))(
            incoming, picker, *depths, *poses
        )
        depths, poses = results[:3], results[3:6]
        if not last:
            sending = results[6]
    return (*depths, *[p.T for p in poses])


def solution(mesh):
    depth = P("view", "edge")
    pose = P(None, ("view", "edge"))
    in_specs = (depth,) * 3 + (pose,) * 3 + (P(), P(("view", "edge"), None, None), P(("view", "edge"), None))
    out_specs = (depth,) * 3 + (pose,) * 3
    return jax.shard_map(shards, mesh=mesh, in_specs=in_specs, out_specs=out_specs, check_vma=False)
```

```python
import functools

import jax
import jax.numpy as jnp
from jax import lax
from jax.experimental import pallas as pl
from jax.experimental.pallas import tpu as pltpu
from jax.sharding import PartitionSpec as P

H = 128
W = 96
ITERS = 2
STEPS_DONE = 10
ROWS = 13
LANES = 128
CAP = 2

learn_rate = 0.01
beta_first = 0.9
beta_second = 0.999
adam_eps = 1e-08

f32 = jnp.float32
bf16 = jnp.bfloat16
EXACT = lax.Precision.HIGHEST


def adam(param, moment, second, half, count, scale):
    moment = beta_first * moment + ((1.0 - beta_first) * scale) * half
    second = beta_second * second + ((1.0 - beta_second) * scale * scale) * (half * half)
    corrected = moment * (learn_rate / (1.0 - beta_first**count))
    spread = second * (1.0 / (1.0 - beta_second**count))
    return (param - corrected / (jnp.sqrt(spread) + adam_eps), moment, second)


def iota(shape, dim):
    return lax.broadcasted_iota(jnp.int32, shape, dim)


def dot(a, b, dims=((1,), (0,)), precision=None):
    return lax.dot_general(a, b, (dims, ((), ())), precision=precision, preferred_element_type=f32)


def fold_matrix():
    return (iota((LANES, LANES), 0) // 8 == iota((LANES, LANES), 1)).astype(f32)


def hot(mask):
    return jnp.where(mask, 1.0, 0.0).astype(bf16)


def make_picker(seconds, start, views):
    lines = seconds.shape[0]
    slots = lines * 8 * CAP
    local = seconds - start
    value = jnp.where((local >= 0) & (local < views), local + 1, 0).astype(f32).astype(bf16)
    row = iota((slots, LANES), 0)
    lane = iota((slots, LANES), 1)
    spread = dot(hot(iota((slots, lines), 0) // (8 * CAP) == iota((slots, lines), 1)), value)
    hit = (spread > 0.5) & (lane // 16 == (row // CAP) % 8)
    tri = hot(iota((LANES, LANES), 0) < iota((LANES, LANES), 1))
    rank = dot(hot(hit), tri)
    mine = hit & (rank == (row % CAP).astype(f32))
    target = jnp.sum(jnp.where(mine, spread, 0.0), axis=1, keepdims=True)
    return hot((iota((slots, views), 1) + 1).astype(f32) == target)


def spread_pose(pose_t):
    lane = iota((8, LANES), 1)
    wide = jnp.zeros((8, LANES), f32)
    for k in range(ROWS):
        wide = jnp.where(lane == iota((8, LANES), 0) + 8 * k, pose_t[:, k : k + 1], wide)
    return jnp.sum(wide, axis=0, keepdims=True)


def gather_pose(row):
    wide = jnp.broadcast_to(row, (8, LANES))
    mine = iota(wide.shape, 1) % 8 == iota(wide.shape, 0)
    return dot(jnp.where(mine, wide, 0.0), fold_matrix()[:, :ROWS], ((1,), (0,)), EXACT)


def two_parts(rows):
    lead = rows.astype(bf16).astype(f32)
    even = iota(rows.shape, 0) % 2 == 0
    return jnp.where(even, lead, rows - lead).astype(bf16)


def send_rows(out, picker, depth, pose_row):
    owners, cap, width = out.shape
    pixels = width - LANES
    picked = dot(picker, depth.astype(bf16)).astype(bf16)
    out[:, :, :pixels] = picked.reshape(owners, cap, pixels)
    wide = jnp.broadcast_to(pose_row, (owners * cap, LANES))
    out[:, :, pixels:] = two_parts(wide).reshape(owners, cap, LANES)


def first_kernel(pairs_hbm, depth_hbm, pose_hbm, out, picker_out, mine, mine_t, pairs, depth, pose_t, sems):
    sources = (pairs_hbm, pose_hbm, depth_hbm)
    copies = [
        pltpu.make_async_copy(src, dst, sems.at[k])
        for k, (src, dst) in enumerate(zip(sources, (pairs, pose_t, depth)))
    ]
    for copy in copies:
        copy.start()
    copies[0].wait()
    views = depth.shape[0]
    picker = make_picker(pairs[:, 1, :], lax.axis_index("view") * views, views)
    picker_out[...] = picker
    copies[1].wait()
    row = spread_pose(pose_t[...])
    copies[2].wait()
    send_rows(out, picker, depth[...], row)

    edges = mine.shape[0]
    me = lax.axis_index("view") * lax.axis_size("edge") + lax.axis_index("edge")
    line = pairs[me // (LANES // edges)].astype(f32)
    lanes = iota((edges, LANES), 1)
    pick = (lanes == me % (LANES // edges) * edges + iota((edges, LANES), 0)).astype(f32)
    for ref, value in (
        (mine, dot(pick, line, ((1,), (1,)), EXACT)),
        (mine_t, dot(line, pick, ((1,), (1,)), EXACT)),
    ):
        ref[...] = (value + 0.5).astype(jnp.int32)


def owner_kernel(count, last, incoming, picker, depth, m, v, pose_t, pose_m, pose_v, *outs):
    owners, cap, width = incoming.shape
    pixels = width - LANES
    grad = dot(picker[...], incoming[:, :, :pixels].reshape(owners * cap, pixels), ((0,), (0,)))
    new = adam(depth[...], m[...], v[...], grad, count, 2.0)
    for ref, value in zip(outs[:3], new):
        ref[...] = value
    rows = incoming[:, :, pixels:].reshape(owners * cap, LANES)
    pose_grad = jnp.sum(rows.astype(f32), axis=0, keepdims=True)
    state = [ref[...] if last else spread_pose(ref[...]) for ref in (pose_t, pose_m, pose_v)]
    new_pose = adam(*state, pose_grad, count, 2.0 / (H * W))
    for ref, value in zip(outs[3:6], new_pose):
        ref[...] = gather_pose(value) if last else value
    if not last:
        send_rows(outs[6], picker[...], new[0], new_pose[0])


def edge_kernel(arrived, mine, mine_t, points, conf, out, depth_s, grad_s):
    groups, shards, cap, width = arrived.shape
    pixels = width - LANES
    edges = mine.shape[0]
    slots = groups * shards * cap

    both = jnp.concatenate([mine[:, 0:1], mine[:, 1:2]], axis=0)
    pose_rows = arrived[:, :, :, pixels:].reshape(slots, LANES)
    slot_of = iota((2 * edges, slots), 1)
    lane_mask = iota((2 * edges, LANES), 1) % 8 == both % 8
    fold = hot(iota((LANES, LANES), 0) // 8 == iota((LANES, LANES), 1))
    poses = None
    for part in range(cap):
        picked = dot(hot(slot_of == both // 8 * cap + part), pose_rows)
        part_poses = dot(jnp.where(lane_mask, picked, 0.0).astype(bf16), fold)
        poses = part_poses if poses is None else poses + part_poses

    group = mine[:, 1:2] // 64
    group_row = mine_t[1:2, :] // 64
    earlier = iota((edges, edges), 1) < iota((edges, edges), 0)
    slot = jnp.sum(jnp.where((group == group_row) & earlier, 1.0, 0.0), axis=1, keepdims=True)
    sel = hot((group * cap).astype(f32) + slot == iota((edges, groups * cap), 1).astype(f32))
    for s in range(shards):
        rows = arrived[:, s, :, :pixels].reshape(groups * cap, pixels)
        depth_s[:, s * pixels : (s + 1) * pixels] = dot(sel, rows)

    pf = [poses[:edges, k : k + 1] for k in range(12)]
    ps = [poses[edges:, k : k + 1] for k in range(13)]
    inv_f = jnp.exp(-ps[12])
    shift = [ps[9 + b] - pf[9 + b] for b in range(3)]
    mix = [[sum(pf[3 * b + a] * ps[3 * b + c] for b in range(3)) for c in range(3)] for a in range(3)]
    base = [sum(pf[3 * b + a] * shift[b] for b in range(3)) for a in range(3)]
    alpha = [mix[a][0] * inv_f for a in range(3)]
    beta = [mix[a][1] * inv_f for a in range(3)]
    tile = (edges, LANES)
    wide_base = [jnp.broadcast_to(x, tile) for x in base]

    period = 3 * LANES
    lines = period // W
    lane = iota((1, LANES), 1)
    us = []
    vs = []
    for k in range(3):
        index = lane + k * LANES
        line = sum((index >= W * (j + 1)).astype(jnp.int32) for j in range(lines - 1))
        us.append((index - line * W).astype(f32) - (W - 1) / 2.0)
        vs.append(line.astype(f32) - (H - 1) / 2.0)
    start = [[alpha[a] * us[k] + (beta[a] * vs[k] + mix[a][2]) for a in range(3)] for k in range(3)]
    slope = [jnp.broadcast_to(beta[a] * float(lines), tile) for a in range(3)]

    def step(i, sums):
        s_acc, d_acc, e_acc = list(sums[:3]), list(sums[3:12]), list(sums[12:])
        rise = [slope[a] * i.astype(f32) for a in range(3)]
        for k in range(3):
            at = pl.ds(pl.multiple_of(i * period + k * LANES, LANES), LANES)
            dep = jnp.exp(depth_s[:, at])
            weight = conf[:, at].astype(f32)
            grad = None
            for a in range(3):
                q = start[k][a] + rise[a]
                r = weight * (dep * q + (wide_base[a] - points[a, :, at].astype(f32)))
                t = r * dep
                grad = t * q if grad is None else grad + t * q
                s_acc[a] = s_acc[a] + r
                d_acc[3 * k + a] = d_acc[3 * k + a] + t
            grad_s[:, at] = grad.astype(bf16)
        for a in range(3):
            e_acc[a] = e_acc[a] + ((d_acc[a] + d_acc[3 + a]) + d_acc[6 + a])
        return (*s_acc, *d_acc, *e_acc)

    steps = shards * pixels // period
    sums = lax.fori_loop(0, steps, step, (jnp.zeros(tile, f32),) * 15)

    def total(x):
        return jnp.sum(x, axis=1, keepdims=True)

    d_acc = sums[3:12]
    d_all = [(d_acc[a] + d_acc[3 + a]) + d_acc[6 + a] for a in range(3)]
    s_sum = [total(x) for x in sums[:3]]
    d_sum = [total(x) for x in d_all]
    u_sum = [total(sum(d_acc[3 * k + a] * us[k] for k in range(3))) for a in range(3)]
    v_sum = [
        total(
            sum(d_acc[3 * k + a] * vs[k] for k in range(3))
            + float(lines) * (float(steps) * d_all[a] - sums[12 + a])
        )
        for a in range(3)
    ]

    for s in range(shards):
        placed = dot(sel, grad_s[:, s * pixels : (s + 1) * pixels], ((0,), (0,))).astype(bf16)
        out[:, s, :, :pixels] = placed.reshape(groups, cap, pixels)

    moments = [[u_sum[a] * inv_f, v_sum[a] * inv_f, d_sum[a]] for a in range(3)]
    grad_first = [None] * 12
    grad_second = [None] * 13
    for b in range(3):
        for a in range(3):
            grad_first[3 * b + a] = sum(ps[3 * b + c] * moments[a][c] for c in range(3)) + shift[b] * s_sum[a]
        for c in range(3):
            grad_second[3 * b + c] = sum(pf[3 * b + a] * moments[a][c] for a in range(3))
        grad_second[9 + b] = sum(pf[3 * b + a] * s_sum[a] for a in range(3))
        grad_first[9 + b] = -grad_second[9 + b]
    grad_second[12] = -sum(alpha[a] * u_sum[a] + beta[a] * v_sum[a] for a in range(3))
    component = iota(tile, 1) // 8
    tables = []
    for grads in (grad_first, grad_second):
        table = jnp.zeros(tile, f32)
        for k, g in enumerate(grads):
            table = jnp.where(component == k, g, table)
        tables.append(table)
    table = jnp.where(lane_mask, jnp.concatenate(tables, axis=0), 0.0)
    lead = table.astype(bf16)
    rest = (table - lead.astype(f32)).astype(bf16)
    both_row = jnp.concatenate([mine_t[0:1, :], mine_t[1:2, :]], axis=1)
    owner_hot = hot(iota((slots, 2 * edges), 0) // cap == both_row // 8)
    owned = dot(owner_hot, lead) + dot(owner_hot, rest)
    out[:, :, :, pixels:] = two_parts(owned).reshape(groups, shards, cap, LANES)


def call(kernel, outs, scratch=(), in_specs=None, mib=40):
    extra = {} if in_specs is None else {"in_specs": in_specs}
    return pl.pallas_call(
        kernel,
        out_shape=outs,
        scratch_shapes=list(scratch),
        compiler_params=pltpu.CompilerParams(vmem_limit_bytes=mib * 1024 * 1024),
        **extra,
    )


def shards(log_depth, depth_m, depth_v, pose, pose_m, pose_v, pairs, points, conf):
    n_view = lax.axis_size("view")
    n_edge = lax.axis_size("edge")
    owners = n_view * n_edge
    views, pixels = log_depth.shape
    edges = points.shape[0]
    width = pixels + LANES

    S = jax.ShapeDtypeStruct
    message = S((owners, CAP, width), bf16)
    depth_out = [S((views, pixels), f32)] * 3
    exchange = functools.partial(
        lax.all_to_all, axis_name=("view", "edge"), split_axis=0, concat_axis=0, tiled=True
    )

    poses = [pose.T, pose_m.T, pose_v.T]
    depths = [log_depth, depth_m, depth_v]
    hbm = pl.BlockSpec(memory_space=pltpu.HBM)
    sending, picker, mine, mine_t = call(
        first_kernel,
        [message, S((owners * CAP, views), bf16), S((edges, 2), jnp.int32), S((2, edges), jnp.int32)],
        [
            pltpu.VMEM((pairs.shape[0] // LANES, 2, LANES), jnp.int32),
            pltpu.VMEM((views, pixels), f32),
            pltpu.VMEM((8, ROWS), f32),
            pltpu.SemaphoreType.DMA((3,)),
        ],
        [hbm, hbm, hbm],
        64,
    )(pairs.T.reshape(2, -1, LANES).transpose(1, 0, 2), log_depth, poses[0])
    planes = points.transpose(1, 0, 2)
    for turn in range(ITERS):
        arrived = exchange(sending).reshape(n_view, n_edge, CAP, width)
        back = call(
            edge_kernel,
            S((n_view, n_edge, CAP, width), bf16),
            [
                pltpu.VMEM((edges, pixels * n_edge), f32),
                pltpu.VMEM((edges, pixels * n_edge), bf16),
            ],
        )(arrived, mine, mine_t, planes, conf)
        incoming = exchange(back.reshape(owners, CAP, width))
        last = turn == ITERS - 1
        kernel = functools.partial(owner_kernel, STEPS_DONE + turn + 1, last)
        pose_out = [S((8, ROWS) if last else (1, LANES), f32)] * 3
        results = call(kernel, depth_out + pose_out + ([] if last else [message]))(
            incoming, picker, *depths, *poses
        )
        depths, poses = results[:3], results[3:6]
        if not last:
            sending = results[6]
    return (*depths, *[p.T for p in poses])


def solution(mesh):
    depth = P("view", "edge")
    pose = P(None, ("view", "edge"))
    in_specs = (depth,) * 3 + (pose,) * 3 + (P(), P(("view", "edge"), None, None), P(("view", "edge"), None))
    out_specs = (depth,) * 3 + (pose,) * 3
    return jax.shard_map(shards, mesh=mesh, in_specs=in_specs, out_specs=out_specs, check_vma=False)
```

```python
import functools

import jax
import jax.numpy as jnp
from jax import lax
from jax.experimental import pallas as pl
from jax.experimental.pallas import tpu as pltpu
from jax.sharding import PartitionSpec as P

H = 128
W = 96
ITERS = 2
STEPS_DONE = 10
ROWS = 13
LANES = 128
CAP = 2

learn_rate = 0.01
beta_first = 0.9
beta_second = 0.999
adam_eps = 1e-08

f32 = jnp.float32
bf16 = jnp.bfloat16
EXACT = lax.Precision.HIGHEST


def adam(param, moment, second, half, count, scale):
    moment = beta_first * moment + ((1.0 - beta_first) * scale) * half
    second = beta_second * second + ((1.0 - beta_second) * scale * scale) * (half * half)
    corrected = moment * (learn_rate / (1.0 - beta_first**count))
    spread = second * (1.0 / (1.0 - beta_second**count))
    return (param - corrected / (jnp.sqrt(spread) + adam_eps), moment, second)


def iota(shape, dim):
    return lax.broadcasted_iota(jnp.int32, shape, dim)


def dot(a, b, dims=((1,), (0,)), precision=None):
    return lax.dot_general(a, b, (dims, ((), ())), precision=precision, preferred_element_type=f32)


def fold_matrix():
    return (iota((LANES, LANES), 0) // 8 == iota((LANES, LANES), 1)).astype(f32)


def hot(mask):
    return jnp.where(mask, 1.0, 0.0).astype(bf16)


def make_picker(seconds, start, views):
    lines = seconds.shape[0]
    slots = lines * 8 * CAP
    local = seconds - start
    value = jnp.where((local >= 0) & (local < views), local + 1, 0).astype(f32).astype(bf16)
    row = iota((slots, LANES), 0)
    lane = iota((slots, LANES), 1)
    spread = dot(hot(iota((slots, lines), 0) // (8 * CAP) == iota((slots, lines), 1)), value)
    hit = (spread > 0.5) & (lane // 16 == (row // CAP) % 8)
    tri = hot(iota((LANES, LANES), 0) < iota((LANES, LANES), 1))
    rank = dot(hot(hit), tri)
    mine = hit & (rank == (row % CAP).astype(f32))
    target = jnp.sum(jnp.where(mine, spread, 0.0), axis=1, keepdims=True)
    return hot((iota((slots, views), 1) + 1).astype(f32) == target)


def spread_pose(pose_t):
    lane = iota((8, LANES), 1)
    wide = jnp.zeros((8, LANES), f32)
    for k in range(ROWS):
        wide = jnp.where(lane == iota((8, LANES), 0) + 8 * k, pose_t[:, k : k + 1], wide)
    return jnp.sum(wide, axis=0, keepdims=True)


def gather_pose(row):
    wide = jnp.broadcast_to(row, (8, LANES))
    mine = iota(wide.shape, 1) % 8 == iota(wide.shape, 0)
    return dot(jnp.where(mine, wide, 0.0), fold_matrix()[:, :ROWS], ((1,), (0,)), EXACT)


def two_parts(rows):
    lead = rows.astype(bf16).astype(f32)
    even = iota(rows.shape, 0) % 2 == 0
    return jnp.where(even, lead, rows - lead).astype(bf16)


def send_rows(out, picker, depth, pose_row):
    owners, cap, width = out.shape
    pixels = width - LANES
    picked = dot(picker, depth.astype(bf16)).astype(bf16)
    out[:, :, :pixels] = picked.reshape(owners, cap, pixels)
    wide = jnp.broadcast_to(pose_row, (owners * cap, LANES))
    out[:, :, pixels:] = two_parts(wide).reshape(owners, cap, LANES)


def first_kernel(
    pairs_hbm, depth_hbm, pose_hbm, out_hbm, picker_out, mine, mine_t, pairs, depth, pose_t, out, sems, out_sems
):
    sources = (pairs_hbm, pose_hbm, depth_hbm)
    copies = [
        pltpu.make_async_copy(src, dst, sems.at[k])
        for k, (src, dst) in enumerate(zip(sources, (pairs, pose_t, depth)))
    ]
    for copy in copies:
        copy.start()
    copies[0].wait()
    views = depth.shape[0]
    edges = mine.shape[0]
    me = lax.axis_index("view") * lax.axis_size("edge") + lax.axis_index("edge")
    line = pairs[me // (LANES // edges)].astype(f32)
    lanes = iota((edges, LANES), 1)
    pick = (lanes == me % (LANES // edges) * edges + iota((edges, LANES), 0)).astype(f32)
    for ref, value in (
        (mine, dot(pick, line, ((1,), (1,)), EXACT)),
        (mine_t, dot(line, pick, ((1,), (1,)), EXACT)),
    ):
        ref[...] = (value + 0.5).astype(jnp.int32)

    picker = make_picker(pairs[:, 1, :], lax.axis_index("view") * views, views)
    picker_out[...] = picker
    copies[1].wait()
    owners, cap, width = out.shape
    pixels = width - LANES
    wide = jnp.broadcast_to(spread_pose(pose_t[...]), (owners * cap, LANES))
    out[:, :, pixels:] = two_parts(wide).reshape(owners, cap, LANES)
    copies[2].wait()
    rounded = depth[...].astype(bf16)
    pieces = out_sems.shape[0]
    step = owners // pieces
    sends = []
    for n in range(pieces):
        part = pl.ds(n * step, step)
        picked = dot(picker[n * step * cap : (n + 1) * step * cap], rounded).astype(bf16)
        out[part, :, :pixels] = picked.reshape(step, cap, pixels)
        sends.append(pltpu.make_async_copy(out.at[part], out_hbm.at[part], out_sems.at[n]))
        sends[-1].start()
    for send in sends:
        send.wait()


def depth_grad(incoming, picker):
    owners, cap, width = incoming.shape
    pixels = width - LANES
    return dot(picker[...], incoming[:, :, :pixels].reshape(owners * cap, pixels), ((0,), (0,)))


def pose_update(incoming, state, count):
    owners, cap, width = incoming.shape
    rows = incoming[:, :, width - LANES :].reshape(owners * cap, LANES)
    grad = jnp.sum(rows.astype(f32), axis=0, keepdims=True)
    return adam(*state, grad, count, 2.0 / (H * W))


def owner_kernel(count, incoming, picker, depth, m, v, pose_t, pose_m, pose_v, *outs):
    new = adam(depth[...], m[...], v[...], depth_grad(incoming, picker), count, 2.0)
    for ref, value in zip(outs[:3], new):
        ref[...] = value
    new_pose = pose_update(incoming, [spread_pose(ref[...]) for ref in (pose_t, pose_m, pose_v)], count)
    for ref, value in zip(outs[3:6], new_pose):
        ref[...] = value
    send_rows(outs[6], picker[...], new[0], new_pose[0])


def last_kernel(count, incoming, picker, depth, m, v, pose, pose_m, pose_v, *refs):
    targets, pose_outs, parts, grad_s, sems = refs[:3], refs[3:6], refs[6:9], refs[9], refs[10]
    grad_s[...] = depth_grad(incoming, picker)
    pieces = sems.shape[1]
    step = depth.shape[0] // pieces
    sends = []
    for n in range(pieces):
        rows = pl.ds(n * step, step)
        new = adam(depth[rows, :], m[rows, :], v[rows, :], grad_s[rows, :], count, 2.0)
        for k, value in enumerate(new):
            parts[k][rows, :] = value
            send = pltpu.make_async_copy(parts[k].at[rows, :], targets[k].at[rows, :], sems.at[k, n])
            send.start()
            sends.append(send)
    new_pose = pose_update(incoming, [ref[...] for ref in (pose, pose_m, pose_v)], count)
    for ref, value in zip(pose_outs, new_pose):
        ref[...] = gather_pose(value)
    for send in sends:
        send.wait()


def edge_kernel(arrived, mine, mine_t, points, conf, out, depth_s, grad_s):
    groups, shards, cap, width = arrived.shape
    pixels = width - LANES
    edges = mine.shape[0]
    slots = groups * shards * cap

    both = jnp.concatenate([mine[:, 0:1], mine[:, 1:2]], axis=0)
    pose_rows = arrived[:, :, :, pixels:].reshape(slots, LANES)
    slot_of = iota((2 * edges, slots), 1)
    lane_mask = iota((2 * edges, LANES), 1) % 8 == both % 8
    fold = hot(iota((LANES, LANES), 0) // 8 == iota((LANES, LANES), 1))
    poses = None
    for part in range(cap):
        picked = dot(hot(slot_of == both // 8 * cap + part), pose_rows)
        part_poses = dot(jnp.where(lane_mask, picked, 0.0).astype(bf16), fold)
        poses = part_poses if poses is None else poses + part_poses

    group = mine[:, 1:2] // 64
    group_row = mine_t[1:2, :] // 64
    earlier = iota((edges, edges), 1) < iota((edges, edges), 0)
    slot = jnp.sum(jnp.where((group == group_row) & earlier, 1.0, 0.0), axis=1, keepdims=True)
    sel = hot((group * cap).astype(f32) + slot == iota((edges, groups * cap), 1).astype(f32))
    for s in range(shards):
        rows = arrived[:, s, :, :pixels].reshape(groups * cap, pixels)
        depth_s[:, s * pixels : (s + 1) * pixels] = jnp.exp(dot(sel, rows))

    pf = [poses[:edges, k : k + 1] for k in range(12)]
    ps = [poses[edges:, k : k + 1] for k in range(13)]
    inv_f = jnp.exp(-ps[12])
    shift = [ps[9 + b] - pf[9 + b] for b in range(3)]
    mix = [[sum(pf[3 * b + a] * ps[3 * b + c] for b in range(3)) for c in range(3)] for a in range(3)]
    base = [sum(pf[3 * b + a] * shift[b] for b in range(3)) for a in range(3)]
    alpha = [mix[a][0] * inv_f for a in range(3)]
    beta = [mix[a][1] * inv_f for a in range(3)]
    tile = (edges, LANES)
    wide_base = [jnp.broadcast_to(x, tile) for x in base]

    period = 3 * LANES
    lines = period // W
    lane = iota((1, LANES), 1)
    us = []
    vs = []
    for k in range(3):
        index = lane + k * LANES
        line = sum((index >= W * (j + 1)).astype(jnp.int32) for j in range(lines - 1))
        us.append((index - line * W).astype(f32) - (W - 1) / 2.0)
        vs.append(line.astype(f32) - (H - 1) / 2.0)
    start = [[alpha[a] * us[k] + (beta[a] * vs[k] + mix[a][2]) for a in range(3)] for k in range(3)]
    slope = [jnp.broadcast_to(beta[a] * float(lines), tile) for a in range(3)]

    def step(i, sums):
        s_acc, d_acc, e_acc = list(sums[:3]), list(sums[3:12]), list(sums[12:])
        rise = [slope[a] * i.astype(f32) for a in range(3)]
        for k in range(3):
            at = pl.ds(pl.multiple_of(i * period + k * LANES, LANES), LANES)
            dep = depth_s[:, at]
            weight = conf[:, at].astype(f32)
            grad = None
            for a in range(3):
                q = start[k][a] + rise[a]
                r = weight * (dep * q + (wide_base[a] - points[a, :, at].astype(f32)))
                t = r * dep
                grad = t * q if grad is None else grad + t * q
                s_acc[a] = s_acc[a] + r
                d_acc[3 * k + a] = d_acc[3 * k + a] + t
            grad_s[:, at] = grad.astype(bf16)
        for a in range(3):
            e_acc[a] = e_acc[a] + ((d_acc[a] + d_acc[3 + a]) + d_acc[6 + a])
        return (*s_acc, *d_acc, *e_acc)

    steps = shards * pixels // period
    sums = lax.fori_loop(0, steps, step, (jnp.zeros(tile, f32),) * 15, unroll=4)

    def total(x):
        return jnp.sum(x, axis=1, keepdims=True)

    d_acc = sums[3:12]
    d_all = [(d_acc[a] + d_acc[3 + a]) + d_acc[6 + a] for a in range(3)]
    s_sum = [total(x) for x in sums[:3]]
    d_sum = [total(x) for x in d_all]
    u_sum = [total(sum(d_acc[3 * k + a] * us[k] for k in range(3))) for a in range(3)]
    v_sum = [
        total(
            sum(d_acc[3 * k + a] * vs[k] for k in range(3))
            + float(lines) * (float(steps) * d_all[a] - sums[12 + a])
        )
        for a in range(3)
    ]

    for s in range(shards):
        placed = dot(sel, grad_s[:, s * pixels : (s + 1) * pixels], ((0,), (0,))).astype(bf16)
        out[:, s, :, :pixels] = placed.reshape(groups, cap, pixels)

    moments = [[u_sum[a] * inv_f, v_sum[a] * inv_f, d_sum[a]] for a in range(3)]
    grad_first = [None] * 12
    grad_second = [None] * 13
    for b in range(3):
        for a in range(3):
            grad_first[3 * b + a] = sum(ps[3 * b + c] * moments[a][c] for c in range(3)) + shift[b] * s_sum[a]
        for c in range(3):
            grad_second[3 * b + c] = sum(pf[3 * b + a] * moments[a][c] for a in range(3))
        grad_second[9 + b] = sum(pf[3 * b + a] * s_sum[a] for a in range(3))
        grad_first[9 + b] = -grad_second[9 + b]
    grad_second[12] = -sum(alpha[a] * u_sum[a] + beta[a] * v_sum[a] for a in range(3))
    component = iota(tile, 1) // 8
    tables = []
    for grads in (grad_first, grad_second):
        table = jnp.zeros(tile, f32)
        for k, g in enumerate(grads):
            table = jnp.where(component == k, g, table)
        tables.append(table)
    table = jnp.where(lane_mask, jnp.concatenate(tables, axis=0), 0.0)
    lead = table.astype(bf16)
    rest = (table - lead.astype(f32)).astype(bf16)
    both_row = jnp.concatenate([mine_t[0:1, :], mine_t[1:2, :]], axis=1)
    owner_hot = hot(iota((slots, 2 * edges), 0) // cap == both_row // 8)
    owned = dot(owner_hot, lead) + dot(owner_hot, rest)
    out[:, :, :, pixels:] = two_parts(owned).reshape(groups, shards, cap, LANES)


def call(kernel, outs, scratch=(), in_specs=None, mib=40, out_specs=None):
    extra = {} if in_specs is None else {"in_specs": in_specs}
    if out_specs is not None:
        extra["out_specs"] = out_specs
    return pl.pallas_call(
        kernel,
        out_shape=outs,
        scratch_shapes=list(scratch),
        compiler_params=pltpu.CompilerParams(vmem_limit_bytes=mib * 1024 * 1024),
        **extra,
    )


def shards(log_depth, depth_m, depth_v, pose, pose_m, pose_v, pairs, points, conf):
    n_view = lax.axis_size("view")
    n_edge = lax.axis_size("edge")
    owners = n_view * n_edge
    views, pixels = log_depth.shape
    edges = points.shape[0]
    width = pixels + LANES

    S = jax.ShapeDtypeStruct
    message = S((owners, CAP, width), bf16)
    depth_out = [S((views, pixels), f32)] * 3
    exchange = functools.partial(
        lax.all_to_all, axis_name=("view", "edge"), split_axis=0, concat_axis=0, tiled=True
    )

    poses = [pose.T, pose_m.T, pose_v.T]
    depths = [log_depth, depth_m, depth_v]
    hbm = pl.BlockSpec(memory_space=pltpu.HBM)
    vmem = pl.BlockSpec(memory_space=pltpu.VMEM)
    sending, picker, mine, mine_t = call(
        first_kernel,
        [message, S((owners * CAP, views), bf16), S((edges, 2), jnp.int32), S((2, edges), jnp.int32)],
        [
            pltpu.VMEM((pairs.shape[0] // LANES, 2, LANES), jnp.int32),
            pltpu.VMEM((views, pixels), f32),
            pltpu.VMEM((8, ROWS), f32),
            pltpu.VMEM((owners, CAP, width), bf16),
            pltpu.SemaphoreType.DMA((3,)),
            pltpu.SemaphoreType.DMA((4,)),
        ],
        [hbm, hbm, hbm],
        64,
        [hbm, vmem, vmem, vmem],
    )(pairs.T.reshape(2, -1, LANES).transpose(1, 0, 2), log_depth, poses[0])
    planes = points.transpose(1, 0, 2)
    for turn in range(ITERS):
        arrived = exchange(sending).reshape(n_view, n_edge, CAP, width)
        back = call(
            edge_kernel,
            S((n_view, n_edge, CAP, width), bf16),
            [
                pltpu.VMEM((edges, pixels * n_edge), f32),
                pltpu.VMEM((edges, pixels * n_edge), bf16),
            ],
        )(arrived, mine, mine_t, planes, conf)
        incoming = exchange(back.reshape(owners, CAP, width))
        count = STEPS_DONE + turn + 1
        if turn < ITERS - 1:
            results = call(
                functools.partial(owner_kernel, count),
                depth_out + [S((1, LANES), f32)] * 3 + [message],
            )(incoming, picker, *depths, *poses)
            sending = results[6]
        else:
            results = call(
                functools.partial(last_kernel, count),
                depth_out + [S((8, ROWS), f32)] * 3,
                [pltpu.VMEM((views, pixels), f32)] * 4 + [pltpu.SemaphoreType.DMA((3, 4))],
                out_specs=[hbm] * 3 + [vmem] * 3,
            )(incoming, picker, *depths, *poses)
        depths, poses = results[:3], results[3:6]
    return (*depths, *[p.T for p in poses])


def solution(mesh):
    depth = P("view", "edge")
    pose = P(None, ("view", "edge"))
    in_specs = (depth,) * 3 + (pose,) * 3 + (P(), P(("view", "edge"), None, None), P(("view", "edge"), None))
    out_specs = (depth,) * 3 + (pose,) * 3
    return jax.shard_map(shards, mesh=mesh, in_specs=in_specs, out_specs=out_specs, check_vma=False)
```

```python
import functools

import jax
import jax.numpy as jnp
from jax import lax
from jax.experimental import pallas as pl
from jax.experimental.pallas import tpu as pltpu
from jax.sharding import PartitionSpec as P

H = 128
W = 96
ITERS = 2
STEPS_DONE = 10
ROWS = 13
LANES = 128
CAP = 2

learn_rate = 0.01
beta_first = 0.9
beta_second = 0.999
adam_eps = 1e-08

f32 = jnp.float32
bf16 = jnp.bfloat16
EXACT = lax.Precision.HIGHEST


def adam(param, moment, second, half, count, scale):
    moment = beta_first * moment + ((1.0 - beta_first) * scale) * half
    second = beta_second * second + ((1.0 - beta_second) * scale * scale) * (half * half)
    corrected = moment * (learn_rate / (1.0 - beta_first**count))
    spread = second * (1.0 / (1.0 - beta_second**count))
    return (param - corrected / (jnp.sqrt(spread) + adam_eps), moment, second)


def iota(shape, dim):
    return lax.broadcasted_iota(jnp.int32, shape, dim)


def dot(a, b, dims=((1,), (0,)), precision=None):
    return lax.dot_general(a, b, (dims, ((), ())), precision=precision, preferred_element_type=f32)


def fold_matrix():
    return (iota((LANES, LANES), 0) // 8 == iota((LANES, LANES), 1)).astype(f32)


def hot(mask):
    return jnp.where(mask, 1.0, 0.0).astype(bf16)


def make_picker(seconds, start, views):
    lines = seconds.shape[0]
    slots = lines * 8 * CAP
    local = seconds - start
    value = jnp.where((local >= 0) & (local < views), local + 1, 0).astype(f32).astype(bf16)
    row = iota((slots, LANES), 0)
    lane = iota((slots, LANES), 1)
    spread = dot(hot(row[:, :lines] // CAP % lines == lane[:, :lines]), value)
    hit = (spread > 0.5) & (lane // 16 == row // (CAP * lines))
    tri = hot(iota((LANES, LANES), 0) < iota((LANES, LANES), 1))
    rank = dot(hot(hit), tri)
    mine = hit & (rank == (row % CAP).astype(f32))
    target = jnp.sum(jnp.where(mine, spread, 0.0), axis=1, keepdims=True)
    return hot((iota((slots, views), 1) + 1).astype(f32) == target)


def spread_pose(pose_t):
    lane = iota((8, LANES), 1)
    wide = jnp.zeros((8, LANES), f32)
    for k in range(ROWS):
        wide = jnp.where(lane == iota((8, LANES), 0) + 8 * k, pose_t[:, k : k + 1], wide)
    return jnp.sum(wide, axis=0, keepdims=True)


def gather_pose(row):
    wide = jnp.broadcast_to(row, (8, LANES))
    mine = iota(wide.shape, 1) % 8 == iota(wide.shape, 0)
    return dot(jnp.where(mine, wide, 0.0), fold_matrix()[:, :ROWS], ((1,), (0,)), EXACT)


def two_parts(rows):
    lead = rows.astype(bf16).astype(f32)
    even = iota(rows.shape, 0) % 2 == 0
    return jnp.where(even, lead, rows - lead).astype(bf16)


def send_rows(out, picker, depth, pose_row):
    owners, cap, width = out.shape
    pixels = width - LANES
    picked = dot(picker, depth.astype(bf16)).astype(bf16)
    out[:, :, :pixels] = picked.reshape(owners, cap, pixels)
    wide = jnp.broadcast_to(pose_row, (owners * cap, LANES))
    out[:, :, pixels:] = two_parts(wide).reshape(owners, cap, LANES)


def first_kernel(pairs_hbm, depth_hbm, pose_hbm, out, picker_out, mine, mine_t, pairs, depth, pose_t, sems):
    sources = (pairs_hbm, pose_hbm, depth_hbm)
    copies = [
        pltpu.make_async_copy(src, dst, sems.at[k])
        for k, (src, dst) in enumerate(zip(sources, (pairs, pose_t, depth)))
    ]
    for copy in copies:
        copy.start()
    copies[0].wait()
    views = depth.shape[0]
    picker = make_picker(pairs[:, 1, :], lax.axis_index("view") * views, views)
    picker_out[...] = picker
    copies[1].wait()
    row = spread_pose(pose_t[...])
    copies[2].wait()
    send_rows(out, picker, depth[...], row)

    edges = mine.shape[0]
    me = lax.axis_index("view") * lax.axis_size("edge") + lax.axis_index("edge")
    line = pairs[me // (LANES // edges)].astype(f32)
    lanes = iota((edges, LANES), 1)
    pick = (lanes == me % (LANES // edges) * edges + iota((edges, LANES), 0)).astype(f32)
    for ref, value in (
        (mine, dot(pick, line, ((1,), (1,)), EXACT)),
        (mine_t, dot(line, pick, ((1,), (1,)), EXACT)),
    ):
        ref[...] = (value + 0.5).astype(jnp.int32)


def owner_kernel(count, last, incoming, picker, depth, m, v, pose_t, pose_m, pose_v, *outs):
    owners, cap, width = incoming.shape
    pixels = width - LANES
    grad = dot(picker[...], incoming[:, :, :pixels].reshape(owners * cap, pixels), ((0,), (0,)))
    new = adam(depth[...], m[...], v[...], grad, count, 2.0)
    for ref, value in zip(outs[:3], new):
        ref[...] = value
    rows = incoming[:, :, pixels:].reshape(owners * cap, LANES)
    pose_grad = jnp.sum(rows.astype(f32), axis=0, keepdims=True)
    state = [ref[...] if last else spread_pose(ref[...]) for ref in (pose_t, pose_m, pose_v)]
    new_pose = adam(*state, pose_grad, count, 2.0 / (H * W))
    for ref, value in zip(outs[3:6], new_pose):
        ref[...] = gather_pose(value) if last else value
    if not last:
        send_rows(outs[6], picker[...], new[0], new_pose[0])


def edge_kernel(arrived, mine, mine_t, points, conf, out, depth_s, grad_s):
    shards, groups, cap, width = arrived.shape
    pixels = width - LANES
    edges = mine.shape[0]
    slots = shards * groups * cap

    def place(view):
        return view // 8 % shards * groups + view // (8 * shards)

    both = jnp.concatenate([mine[:, 0:1], mine[:, 1:2]], axis=0)
    pose_rows = arrived[:, :, :, pixels:].reshape(slots, LANES)
    slot_of = iota((2 * edges, slots), 1)
    lane_mask = iota((2 * edges, LANES), 1) % 8 == both % 8
    fold = hot(iota((LANES, LANES), 0) // 8 == iota((LANES, LANES), 1))
    poses = None
    for part in range(cap):
        picked = dot(hot(slot_of == place(both) * cap + part), pose_rows)
        part_poses = dot(jnp.where(lane_mask, picked, 0.0).astype(bf16), fold)
        poses = part_poses if poses is None else poses + part_poses

    group = mine[:, 1:2] // 64
    group_row = mine_t[1:2, :] // 64
    earlier = iota((edges, edges), 1) < iota((edges, edges), 0)
    slot = jnp.sum(jnp.where((group == group_row) & earlier, 1.0, 0.0), axis=1, keepdims=True)
    sel = hot((group * cap).astype(f32) + slot == iota((edges, groups * cap), 1).astype(f32))
    for s in range(shards):
        rows = arrived[s, :, :, :pixels].reshape(groups * cap, pixels)
        depth_s[:, s * pixels : (s + 1) * pixels] = jnp.exp(dot(sel, rows))

    pf = [poses[:edges, k : k + 1] for k in range(12)]
    ps = [poses[edges:, k : k + 1] for k in range(13)]
    inv_f = jnp.exp(-ps[12])
    shift = [ps[9 + b] - pf[9 + b] for b in range(3)]
    mix = [[sum(pf[3 * b + a] * ps[3 * b + c] for b in range(3)) for c in range(3)] for a in range(3)]
    base = [sum(pf[3 * b + a] * shift[b] for b in range(3)) for a in range(3)]
    alpha = [mix[a][0] * inv_f for a in range(3)]
    beta = [mix[a][1] * inv_f for a in range(3)]
    tile = (edges, LANES)
    wide_base = [jnp.broadcast_to(x, tile) for x in base]

    period = 3 * LANES
    lines = period // W
    lane = iota((1, LANES), 1)
    us = []
    vs = []
    for k in range(3):
        index = lane + k * LANES
        line = sum((index >= W * (j + 1)).astype(jnp.int32) for j in range(lines - 1))
        us.append((index - line * W).astype(f32) - (W - 1) / 2.0)
        vs.append(line.astype(f32) - (H - 1) / 2.0)
    start = [[alpha[a] * us[k] + (beta[a] * vs[k] + mix[a][2]) for a in range(3)] for k in range(3)]
    slope = [jnp.broadcast_to(beta[a] * float(lines), tile) for a in range(3)]

    def step(i, sums):
        s_acc, d_acc, e_acc = list(sums[:3]), list(sums[3:12]), list(sums[12:])
        rise = [slope[a] * i.astype(f32) for a in range(3)]
        for k in range(3):
            at = pl.ds(pl.multiple_of(i * period + k * LANES, LANES), LANES)
            dep = depth_s[:, at]
            weight = conf[:, at].astype(f32)
            grad = None
            for a in range(3):
                q = start[k][a] + rise[a]
                r = weight * (dep * q + (wide_base[a] - points[a, :, at].astype(f32)))
                t = r * dep
                grad = t * q if grad is None else grad + t * q
                s_acc[a] = s_acc[a] + r
                d_acc[3 * k + a] = d_acc[3 * k + a] + t
            grad_s[:, at] = grad.astype(bf16)
        for a in range(3):
            e_acc[a] = e_acc[a] + ((d_acc[a] + d_acc[3 + a]) + d_acc[6 + a])
        return (*s_acc, *d_acc, *e_acc)

    steps = shards * pixels // period
    sums = lax.fori_loop(0, steps, step, (jnp.zeros(tile, f32),) * 15, unroll=4)

    def total(x):
        return jnp.sum(x, axis=1, keepdims=True)

    d_acc = sums[3:12]
    d_all = [(d_acc[a] + d_acc[3 + a]) + d_acc[6 + a] for a in range(3)]
    s_sum = [total(x) for x in sums[:3]]
    d_sum = [total(x) for x in d_all]
    u_sum = [total(sum(d_acc[3 * k + a] * us[k] for k in range(3))) for a in range(3)]
    v_sum = [
        total(
            sum(d_acc[3 * k + a] * vs[k] for k in range(3))
            + float(lines) * (float(steps) * d_all[a] - sums[12 + a])
        )
        for a in range(3)
    ]

    for s in range(shards):
        placed = dot(sel, grad_s[:, s * pixels : (s + 1) * pixels], ((0,), (0,))).astype(bf16)
        out[s, :, :, :pixels] = placed.reshape(groups, cap, pixels)

    moments = [[u_sum[a] * inv_f, v_sum[a] * inv_f, d_sum[a]] for a in range(3)]
    grad_first = [None] * 12
    grad_second = [None] * 13
    for b in range(3):
        for a in range(3):
            grad_first[3 * b + a] = sum(ps[3 * b + c] * moments[a][c] for c in range(3)) + shift[b] * s_sum[a]
        for c in range(3):
            grad_second[3 * b + c] = sum(pf[3 * b + a] * moments[a][c] for a in range(3))
        grad_second[9 + b] = sum(pf[3 * b + a] * s_sum[a] for a in range(3))
        grad_first[9 + b] = -grad_second[9 + b]
    grad_second[12] = -sum(alpha[a] * u_sum[a] + beta[a] * v_sum[a] for a in range(3))
    component = iota(tile, 1) // 8
    tables = []
    for grads in (grad_first, grad_second):
        table = jnp.zeros(tile, f32)
        for k, g in enumerate(grads):
            table = jnp.where(component == k, g, table)
        tables.append(table)
    table = jnp.where(lane_mask, jnp.concatenate(tables, axis=0), 0.0)
    lead = table.astype(bf16)
    rest = (table - lead.astype(f32)).astype(bf16)
    both_row = jnp.concatenate([mine_t[0:1, :], mine_t[1:2, :]], axis=1)
    owner_hot = hot(iota((slots, 2 * edges), 0) // cap == place(both_row))
    owned = dot(owner_hot, lead) + dot(owner_hot, rest)
    out[:, :, :, pixels:] = two_parts(owned).reshape(shards, groups, cap, LANES)


def call(kernel, outs, scratch=(), in_specs=None, mib=40):
    extra = {} if in_specs is None else {"in_specs": in_specs}
    return pl.pallas_call(
        kernel,
        out_shape=outs,
        scratch_shapes=list(scratch),
        compiler_params=pltpu.CompilerParams(vmem_limit_bytes=mib * 1024 * 1024),
        **extra,
    )


def shards(log_depth, depth_m, depth_v, pose, pose_m, pose_v, pairs, points, conf):
    n_view = lax.axis_size("view")
    n_edge = lax.axis_size("edge")
    owners = n_view * n_edge
    views, pixels = log_depth.shape
    edges = points.shape[0]
    width = pixels + LANES

    S = jax.ShapeDtypeStruct
    message = S((owners, CAP, width), bf16)
    depth_out = [S((views, pixels), f32)] * 3
    exchange = functools.partial(
        lax.all_to_all, axis_name=("edge", "view"), split_axis=0, concat_axis=0, tiled=True
    )

    poses = [pose.T, pose_m.T, pose_v.T]
    depths = [log_depth, depth_m, depth_v]
    hbm = pl.BlockSpec(memory_space=pltpu.HBM)
    sending, picker, mine, mine_t = call(
        first_kernel,
        [message, S((owners * CAP, views), bf16), S((edges, 2), jnp.int32), S((2, edges), jnp.int32)],
        [
            pltpu.VMEM((pairs.shape[0] // LANES, 2, LANES), jnp.int32),
            pltpu.VMEM((views, pixels), f32),
            pltpu.VMEM((8, ROWS), f32),
            pltpu.SemaphoreType.DMA((3,)),
        ],
        [hbm, hbm, hbm],
        64,
    )(pairs.T.reshape(2, -1, LANES).transpose(1, 0, 2), log_depth, poses[0])
    planes = points.transpose(1, 0, 2)
    for turn in range(ITERS):
        arrived = exchange(sending).reshape(n_edge, n_view, CAP, width)
        back = call(
            edge_kernel,
            S((n_edge, n_view, CAP, width), bf16),
            [
                pltpu.VMEM((edges, pixels * n_edge), f32),
                pltpu.VMEM((edges, pixels * n_edge), bf16),
            ],
        )(arrived, mine, mine_t, planes, conf)
        incoming = exchange(back.reshape(owners, CAP, width))
        last = turn == ITERS - 1
        kernel = functools.partial(owner_kernel, STEPS_DONE + turn + 1, last)
        pose_out = [S((8, ROWS) if last else (1, LANES), f32)] * 3
        results = call(kernel, depth_out + pose_out + ([] if last else [message]))(
            incoming, picker, *depths, *poses
        )
        depths, poses = results[:3], results[3:6]
        if not last:
            sending = results[6]
    return (*depths, *[p.T for p in poses])


def solution(mesh):
    depth = P("view", "edge")
    pose = P(None, ("view", "edge"))
    in_specs = (depth,) * 3 + (pose,) * 3 + (P(), P(("view", "edge"), None, None), P(("view", "edge"), None))
    out_specs = (depth,) * 3 + (pose,) * 3
    return jax.shard_map(shards, mesh=mesh, in_specs=in_specs, out_specs=out_specs, check_vma=False)
```

```python
import functools

import jax
import jax.numpy as jnp
from jax import lax
from jax.experimental import pallas as pl
from jax.experimental.pallas import tpu as pltpu
from jax.sharding import PartitionSpec as P

H = 128
W = 96
ITERS = 2
STEPS_DONE = 10
ROWS = 13
LANES = 128
CAP = 2
CORES = 2
SHARDS = 8
ORDER = ("z", "x", "y", "core")

learn_rate = 0.01
beta_first = 0.9
beta_second = 0.999
adam_eps = 1e-08

f32 = jnp.float32
bf16 = jnp.bfloat16
EXACT = lax.Precision.HIGHEST


def adam(param, moment, second, half, count, scale):
    moment = beta_first * moment + ((1.0 - beta_first) * scale) * half
    second = beta_second * second + ((1.0 - beta_second) * scale * scale) * (half * half)
    corrected = moment * (learn_rate / (1.0 - beta_first**count))
    spread = second * (1.0 / (1.0 - beta_second**count))
    return (param - corrected / (jnp.sqrt(spread) + adam_eps), moment, second)


def iota(shape, dim):
    return lax.broadcasted_iota(jnp.int32, shape, dim)


def dot(a, b, dims=((1,), (0,)), precision=None):
    return lax.dot_general(a, b, (dims, ((), ())), precision=precision, preferred_element_type=f32)


def fold_matrix():
    return (iota((LANES, LANES), 0) // 8 == iota((LANES, LANES), 1)).astype(f32)


def hot(mask):
    return jnp.where(mask, 1.0, 0.0).astype(bf16)


def make_picker(seconds, start, views):
    lines = seconds.shape[0]
    slots = lines * 8 * CAP
    local = seconds - start
    value = jnp.where((local >= 0) & (local < views), local + 1, 0).astype(f32).astype(bf16)
    row = iota((slots, LANES), 0)
    lane = iota((slots, LANES), 1)
    spread = dot(hot(row[:, :lines] // (CAP * CORES) % lines == lane[:, :lines]), value)
    place = row // CAP
    shard = place // (CORES * lines) * CORES + place % CORES
    hit = (spread > 0.5) & (lane // 16 == shard)
    tri = hot(iota((LANES, LANES), 0) < iota((LANES, LANES), 1))
    rank = dot(hot(hit), tri)
    mine = hit & (rank == (row % CAP).astype(f32))
    target = jnp.sum(jnp.where(mine, spread, 0.0), axis=1, keepdims=True)
    return hot((iota((slots, views), 1) + 1).astype(f32) == target)


def spread_pose(pose_t):
    lane = iota((8, LANES), 1)
    wide = jnp.zeros((8, LANES), f32)
    for k in range(ROWS):
        wide = jnp.where(lane == iota((8, LANES), 0) + 8 * k, pose_t[:, k : k + 1], wide)
    return jnp.sum(wide, axis=0, keepdims=True)


def gather_pose(row):
    wide = jnp.broadcast_to(row, (8, LANES))
    mine = iota(wide.shape, 1) % 8 == iota(wide.shape, 0)
    return dot(jnp.where(mine, wide, 0.0), fold_matrix()[:, :ROWS], ((1,), (0,)), EXACT)


def two_parts(rows):
    lead = rows.astype(bf16).astype(f32)
    even = iota(rows.shape, 0) % 2 == 0
    return jnp.where(even, lead, rows - lead).astype(bf16)


def send_rows(out, picker, depth, pose_row):
    owners, cap, width = out.shape
    pixels = width - LANES
    picked = dot(picker, depth.astype(bf16)).astype(bf16)
    out[:, :, :pixels] = picked.reshape(owners, cap, pixels)
    wide = jnp.broadcast_to(pose_row, (owners * cap, LANES))
    out[:, :, pixels:] = two_parts(wide).reshape(owners, cap, LANES)


def first_kernel(pairs_hbm, depth_hbm, pose_hbm, out, picker_out, mine, mine_t, pairs, depth, pose_t, sems):
    sources = (pairs_hbm, pose_hbm, depth_hbm)
    copies = [
        pltpu.make_async_copy(src, dst, sems.at[k])
        for k, (src, dst) in enumerate(zip(sources, (pairs, pose_t, depth)))
    ]
    for copy in copies:
        copy.start()
    copies[0].wait()
    views = depth.shape[0]
    picker = make_picker(pairs[:, 1, :], lax.axis_index(("x", "y")) * views, views)
    picker_out[...] = picker
    copies[1].wait()
    row = spread_pose(pose_t[...])
    copies[2].wait()
    send_rows(out, picker, depth[...], row)

    edges = mine.shape[0]
    me = lax.axis_index(("x", "y")) * SHARDS + lax.axis_index(("z", "core"))
    line = pairs[me // (LANES // edges)].astype(f32)
    lanes = iota((edges, LANES), 1)
    pick = (lanes == me % (LANES // edges) * edges + iota((edges, LANES), 0)).astype(f32)
    for ref, value in (
        (mine, dot(pick, line, ((1,), (1,)), EXACT)),
        (mine_t, dot(line, pick, ((1,), (1,)), EXACT)),
    ):
        ref[...] = (value + 0.5).astype(jnp.int32)


def owner_kernel(count, last, incoming, picker, depth, m, v, pose_t, pose_m, pose_v, *outs):
    owners, cap, width = incoming.shape
    pixels = width - LANES
    grad = dot(picker[...], incoming[:, :, :pixels].reshape(owners * cap, pixels), ((0,), (0,)))
    new = adam(depth[...], m[...], v[...], grad, count, 2.0)
    for ref, value in zip(outs[:3], new):
        ref[...] = value
    rows = incoming[:, :, pixels:].reshape(owners * cap, LANES)
    pose_grad = jnp.sum(rows.astype(f32), axis=0, keepdims=True)
    state = [ref[...] if last else spread_pose(ref[...]) for ref in (pose_t, pose_m, pose_v)]
    new_pose = adam(*state, pose_grad, count, 2.0 / (H * W))
    for ref, value in zip(outs[3:6], new_pose):
        ref[...] = gather_pose(value) if last else value
    if not last:
        send_rows(outs[6], picker[...], new[0], new_pose[0])


def edge_kernel(arrived, mine, mine_t, points, conf, out, depth_s, grad_s):
    planes, groups, cores, cap, width = arrived.shape
    shards = planes * cores
    pixels = width - LANES
    edges = mine.shape[0]
    slots = shards * groups * cap

    def place(view):
        shard = view // 8 % shards
        return (shard // cores * groups + view // (8 * shards)) * cores + shard % cores

    both = jnp.concatenate([mine[:, 0:1], mine[:, 1:2]], axis=0)
    pose_rows = arrived[:, :, :, :, pixels:].reshape(slots, LANES)
    slot_of = iota((2 * edges, slots), 1)
    lane_mask = iota((2 * edges, LANES), 1) % 8 == both % 8
    fold = hot(iota((LANES, LANES), 0) // 8 == iota((LANES, LANES), 1))
    poses = None
    for part in range(cap):
        picked = dot(hot(slot_of == place(both) * cap + part), pose_rows)
        part_poses = dot(jnp.where(lane_mask, picked, 0.0).astype(bf16), fold)
        poses = part_poses if poses is None else poses + part_poses

    group = mine[:, 1:2] // 64
    group_row = mine_t[1:2, :] // 64
    earlier = iota((edges, edges), 1) < iota((edges, edges), 0)
    slot = jnp.sum(jnp.where((group == group_row) & earlier, 1.0, 0.0), axis=1, keepdims=True)
    sel = hot((group * cap).astype(f32) + slot == iota((edges, groups * cap), 1).astype(f32))
    for s in range(shards):
        rows = arrived[s // cores, :, s % cores, :, :pixels].reshape(groups * cap, pixels)
        depth_s[:, s * pixels : (s + 1) * pixels] = jnp.exp(dot(sel, rows))

    pf = [poses[:edges, k : k + 1] for k in range(12)]
    ps = [poses[edges:, k : k + 1] for k in range(13)]
    inv_f = jnp.exp(-ps[12])
    shift = [ps[9 + b] - pf[9 + b] for b in range(3)]
    mix = [[sum(pf[3 * b + a] * ps[3 * b + c] for b in range(3)) for c in range(3)] for a in range(3)]
    base = [sum(pf[3 * b + a] * shift[b] for b in range(3)) for a in range(3)]
    alpha = [mix[a][0] * inv_f for a in range(3)]
    beta = [mix[a][1] * inv_f for a in range(3)]
    tile = (edges, LANES)
    wide_base = [jnp.broadcast_to(x, tile) for x in base]

    period = 3 * LANES
    lines = period // W
    lane = iota((1, LANES), 1)
    us = []
    vs = []
    for k in range(3):
        index = lane + k * LANES
        line = sum((index >= W * (j + 1)).astype(jnp.int32) for j in range(lines - 1))
        us.append((index - line * W).astype(f32) - (W - 1) / 2.0)
        vs.append(line.astype(f32) - (H - 1) / 2.0)
    start = [[alpha[a] * us[k] + (beta[a] * vs[k] + mix[a][2]) for a in range(3)] for k in range(3)]
    slope = [jnp.broadcast_to(beta[a] * float(lines), tile) for a in range(3)]

    def step(i, sums):
        s_acc, d_acc, e_acc = list(sums[:3]), list(sums[3:12]), list(sums[12:])
        rise = [slope[a] * float(i) for a in range(3)]
        for k in range(3):
            at = pl.ds(i * period + k * LANES, LANES)
            dep = depth_s[:, at]
            weight = conf[:, at].astype(f32)
            grad = None
            for a in range(3):
                q = start[k][a] + rise[a]
                r = weight * (dep * q + (wide_base[a] - points[a, :, at].astype(f32)))
                t = r * dep
                grad = t * q if grad is None else grad + t * q
                s_acc[a] = s_acc[a] + r
                d_acc[3 * k + a] = d_acc[3 * k + a] + t
            grad_s[:, at] = grad.astype(bf16)
        for a in range(3):
            e_acc[a] = e_acc[a] + ((d_acc[a] + d_acc[3 + a]) + d_acc[6 + a])
        return (*s_acc, *d_acc, *e_acc)

    steps = shards * pixels // period
    sums = (jnp.zeros(tile, f32),) * 15
    for s in range(shards):
        for i in range(steps // shards):
            sums = step(s * (steps // shards) + i, sums)
        placed = dot(sel, grad_s[:, s * pixels : (s + 1) * pixels], ((0,), (0,))).astype(bf16)
        out[s // cores, :, s % cores, :, :pixels] = placed.reshape(groups, cap, pixels)

    def total(x):
        return jnp.sum(x, axis=1, keepdims=True)

    d_acc = sums[3:12]
    d_all = [(d_acc[a] + d_acc[3 + a]) + d_acc[6 + a] for a in range(3)]
    s_sum = [total(x) for x in sums[:3]]
    d_sum = [total(x) for x in d_all]
    u_sum = [total(sum(d_acc[3 * k + a] * us[k] for k in range(3))) for a in range(3)]
    v_sum = [
        total(
            sum(d_acc[3 * k + a] * vs[k] for k in range(3))
            + float(lines) * (float(steps) * d_all[a] - sums[12 + a])
        )
        for a in range(3)
    ]

    moments = [[u_sum[a] * inv_f, v_sum[a] * inv_f, d_sum[a]] for a in range(3)]
    grad_first = [None] * 12
    grad_second = [None] * 13
    for b in range(3):
        for a in range(3):
            grad_first[3 * b + a] = sum(ps[3 * b + c] * moments[a][c] for c in range(3)) + shift[b] * s_sum[a]
        for c in range(3):
            grad_second[3 * b + c] = sum(pf[3 * b + a] * moments[a][c] for a in range(3))
        grad_second[9 + b] = sum(pf[3 * b + a] * s_sum[a] for a in range(3))
        grad_first[9 + b] = -grad_second[9 + b]
    grad_second[12] = -sum(alpha[a] * u_sum[a] + beta[a] * v_sum[a] for a in range(3))
    component = iota(tile, 1) // 8
    tables = []
    for grads in (grad_first, grad_second):
        table = jnp.zeros(tile, f32)
        for k, g in enumerate(grads):
            table = jnp.where(component == k, g, table)
        tables.append(table)
    table = jnp.where(lane_mask, jnp.concatenate(tables, axis=0), 0.0)
    lead = table.astype(bf16)
    rest = (table - lead.astype(f32)).astype(bf16)
    both_row = jnp.concatenate([mine_t[0:1, :], mine_t[1:2, :]], axis=1)
    owner_hot = hot(iota((slots, 2 * edges), 0) // cap == place(both_row))
    owned = dot(owner_hot, lead) + dot(owner_hot, rest)
    out[:, :, :, :, pixels:] = two_parts(owned).reshape(planes, groups, cores, cap, LANES)


def call(kernel, outs, scratch=(), in_specs=None, mib=40):
    extra = {} if in_specs is None else {"in_specs": in_specs}
    return pl.pallas_call(
        kernel,
        out_shape=outs,
        scratch_shapes=list(scratch),
        compiler_params=pltpu.CompilerParams(vmem_limit_bytes=mib * 1024 * 1024),
        **extra,
    )


def shards(log_depth, depth_m, depth_v, pose, pose_m, pose_v, pairs, points, conf):
    n_view = lax.axis_size("x") * lax.axis_size("y")
    n_edge = lax.axis_size("z") * lax.axis_size("core")
    owners = n_view * n_edge
    views, pixels = log_depth.shape
    edges = points.shape[0]
    width = pixels + LANES

    S = jax.ShapeDtypeStruct
    message = S((owners, CAP, width), bf16)
    depth_out = [S((views, pixels), f32)] * 3
    exchange = functools.partial(
        lax.all_to_all, axis_name=ORDER, split_axis=0, concat_axis=0, tiled=True
    )

    poses = [pose.T, pose_m.T, pose_v.T]
    depths = [log_depth, depth_m, depth_v]
    hbm = pl.BlockSpec(memory_space=pltpu.HBM)
    sending, picker, mine, mine_t = call(
        first_kernel,
        [message, S((owners * CAP, views), bf16), S((edges, 2), jnp.int32), S((2, edges), jnp.int32)],
        [
            pltpu.VMEM((pairs.shape[0] // LANES, 2, LANES), jnp.int32),
            pltpu.VMEM((views, pixels), f32),
            pltpu.VMEM((8, ROWS), f32),
            pltpu.SemaphoreType.DMA((3,)),
        ],
        [hbm, hbm, hbm],
        64,
    )(pairs.T.reshape(2, -1, LANES).transpose(1, 0, 2), log_depth, poses[0])
    planes = points.transpose(1, 0, 2)
    for turn in range(ITERS):
        arrived = exchange(sending).reshape(n_edge // CORES, n_view, CORES, CAP, width)
        back = call(
            edge_kernel,
            S((n_edge // CORES, n_view, CORES, CAP, width), bf16),
            [
                pltpu.VMEM((edges, pixels * n_edge), f32),
                pltpu.VMEM((edges, pixels * n_edge), bf16),
            ],
        )(arrived, mine, mine_t, planes, conf)
        incoming = exchange(back.reshape(owners, CAP, width))
        last = turn == ITERS - 1
        kernel = functools.partial(owner_kernel, STEPS_DONE + turn + 1, last)
        pose_out = [S((8, ROWS) if last else (1, LANES), f32)] * 3
        results = call(kernel, depth_out + pose_out + ([] if last else [message]))(
            incoming, picker, *depths, *poses
        )
        depths, poses = results[:3], results[3:6]
        if not last:
            sending = results[6]
    return (*depths, *[p.T for p in poses])


def solution(mesh):
    grid = jax.sharding.Mesh(mesh.devices.reshape(4, 4, SHARDS // CORES, CORES), ("x", "y", "z", "core"))
    view, edge = ("x", "y"), ("z", "core")
    depth = P(view, edge)
    pose = P(None, view + edge)
    in_specs = (depth,) * 3 + (pose,) * 3 + (P(), P(view + edge, None, None), P(view + edge, None))
    out_specs = (depth,) * 3 + (pose,) * 3
    return jax.shard_map(shards, mesh=grid, in_specs=in_specs, out_specs=out_specs, check_vma=False)
```

```python
import functools

import jax
import jax.numpy as jnp
from jax import lax
from jax.experimental import pallas as pl
from jax.experimental.pallas import tpu as pltpu
from jax.sharding import PartitionSpec as P

H = 128
W = 96
ITERS = 2
STEPS_DONE = 10
ROWS = 13
LANES = 128
CAP = 2

learn_rate = 0.01
beta_first = 0.9
beta_second = 0.999
adam_eps = 1e-08

f32 = jnp.float32
bf16 = jnp.bfloat16
EXACT = lax.Precision.HIGHEST


def adam(param, moment, second, half, count, scale):
    moment = beta_first * moment + ((1.0 - beta_first) * scale) * half
    second = beta_second * second + ((1.0 - beta_second) * scale * scale) * (half * half)
    corrected = moment * (learn_rate / (1.0 - beta_first**count))
    spread = second * (1.0 / (1.0 - beta_second**count))
    return (param - corrected / (jnp.sqrt(spread) + adam_eps), moment, second)


def iota(shape, dim):
    return lax.broadcasted_iota(jnp.int32, shape, dim)


def dot(a, b, dims=((1,), (0,)), precision=None):
    return lax.dot_general(a, b, (dims, ((), ())), precision=precision, preferred_element_type=f32)


def fold_matrix():
    return (iota((LANES, LANES), 0) // 8 == iota((LANES, LANES), 1)).astype(f32)


def hot(mask):
    return jnp.where(mask, 1.0, 0.0).astype(bf16)


def make_picker(seconds, start, views):
    lines = seconds.shape[0]
    slots = lines * 8 * CAP
    local = seconds - start
    value = jnp.where((local >= 0) & (local < views), local + 1, 0).astype(f32).astype(bf16)
    row = iota((slots, LANES), 0)
    lane = iota((slots, LANES), 1)
    spread = dot(hot(row[:, :lines] // CAP % lines == lane[:, :lines]), value)
    hit = (spread > 0.5) & (lane // 16 == row // (CAP * lines))
    tri = hot(iota((LANES, LANES), 0) < iota((LANES, LANES), 1))
    rank = dot(hot(hit), tri)
    mine = hit & (rank == (row % CAP).astype(f32))
    target = jnp.sum(jnp.where(mine, spread, 0.0), axis=1, keepdims=True)
    return hot((iota((slots, views), 1) + 1).astype(f32) == target)


def spread_pose(pose_t):
    lane = iota((8, LANES), 1)
    wide = jnp.zeros((8, LANES), f32)
    for k in range(ROWS):
        wide = jnp.where(lane == iota((8, LANES), 0) + 8 * k, pose_t[:, k : k + 1], wide)
    return jnp.sum(wide, axis=0, keepdims=True)


def gather_pose(row):
    wide = jnp.broadcast_to(row, (8, LANES))
    mine = iota(wide.shape, 1) % 8 == iota(wide.shape, 0)
    return dot(jnp.where(mine, wide, 0.0), fold_matrix()[:, :ROWS], ((1,), (0,)), EXACT)


def two_parts(rows):
    lead = rows.astype(bf16).astype(f32)
    even = iota(rows.shape, 0) % 2 == 0
    return jnp.where(even, lead, rows - lead).astype(bf16)


def send_rows(out, picker, depth, pose_row):
    owners, cap, width = out.shape
    pixels = width - LANES
    picked = dot(picker, depth.astype(bf16)).astype(bf16)
    out[:, :, :pixels] = picked.reshape(owners, cap, pixels)
    wide = jnp.broadcast_to(pose_row, (owners * cap, LANES))
    out[:, :, pixels:] = two_parts(wide).reshape(owners, cap, LANES)


def first_kernel(pairs_hbm, depth_hbm, pose_hbm, out, picker_out, mine, mine_t, pairs, depth, pose_t, sems):
    sources = (pairs_hbm, pose_hbm, depth_hbm)
    copies = [
        pltpu.make_async_copy(src, dst, sems.at[k])
        for k, (src, dst) in enumerate(zip(sources, (pairs, pose_t, depth)))
    ]
    for copy in copies:
        copy.start()
    copies[0].wait()
    views = depth.shape[0]
    picker = make_picker(pairs[:, 1, :], lax.axis_index("view") * views, views)
    picker_out[...] = picker
    copies[1].wait()
    row = spread_pose(pose_t[...])
    copies[2].wait()
    send_rows(out, picker, depth[...], row)

    edges = mine.shape[0]
    me = lax.axis_index("view") * lax.axis_size("edge") + lax.axis_index("edge")
    line = pairs[me // (LANES // edges)].astype(f32)
    lanes = iota((edges, LANES), 1)
    pick = (lanes == me % (LANES // edges) * edges + iota((edges, LANES), 0)).astype(f32)
    for ref, value in (
        (mine, dot(pick, line, ((1,), (1,)), EXACT)),
        (mine_t, dot(line, pick, ((1,), (1,)), EXACT)),
    ):
        ref[...] = (value + 0.5).astype(jnp.int32)


def owner_kernel(count, last, incoming, picker, depth, m, v, pose_t, pose_m, pose_v, *outs):
    owners, cap, width = incoming.shape
    pixels = width - LANES
    grad = dot(picker[...], incoming[:, :, :pixels].reshape(owners * cap, pixels), ((0,), (0,)))
    new = adam(depth[...], m[...], v[...], grad, count, 2.0)
    for ref, value in zip(outs[:3], new):
        ref[...] = value
    rows = incoming[:, :, pixels:].reshape(owners * cap, LANES)
    pose_grad = jnp.sum(rows.astype(f32), axis=0, keepdims=True)
    state = [ref[...] if last else spread_pose(ref[...]) for ref in (pose_t, pose_m, pose_v)]
    new_pose = adam(*state, pose_grad, count, 2.0 / (H * W))
    for ref, value in zip(outs[3:6], new_pose):
        ref[...] = gather_pose(value) if last else value
    if not last:
        send_rows(outs[6], picker[...], new[0], new_pose[0])


def edge_kernel(arrived, mine, mine_t, points, conf, out, depth_s, grad_s):
    shards, groups, cap, width = arrived.shape
    pixels = width - LANES
    edges = mine.shape[0]
    slots = shards * groups * cap

    def place(view):
        return view // 8 % shards * groups + view // (8 * shards)

    both = jnp.concatenate([mine[:, 0:1], mine[:, 1:2]], axis=0)
    pose_rows = arrived[:, :, :, pixels:].reshape(slots, LANES)
    slot_of = iota((2 * edges, slots), 1)
    lane_mask = iota((2 * edges, LANES), 1) % 8 == both % 8
    fold = hot(iota((LANES, LANES), 0) // 8 == iota((LANES, LANES), 1))
    poses = None
    for part in range(cap):
        picked = dot(hot(slot_of == place(both) * cap + part), pose_rows)
        part_poses = dot(jnp.where(lane_mask, picked, 0.0).astype(bf16), fold)
        poses = part_poses if poses is None else poses + part_poses

    group = mine[:, 1:2] // 64
    group_row = mine_t[1:2, :] // 64
    earlier = iota((edges, edges), 1) < iota((edges, edges), 0)
    slot = jnp.sum(jnp.where((group == group_row) & earlier, 1.0, 0.0), axis=1, keepdims=True)
    sel = hot((group * cap).astype(f32) + slot == iota((edges, groups * cap), 1).astype(f32))
    for s in range(shards):
        rows = arrived[s, :, :, :pixels].reshape(groups * cap, pixels)
        depth_s[:, s * pixels : (s + 1) * pixels] = jnp.exp(dot(sel, rows))

    pf = [poses[:edges, k : k + 1] for k in range(12)]
    ps = [poses[edges:, k : k + 1] for k in range(13)]
    inv_f = jnp.exp(-ps[12])
    shift = [ps[9 + b] - pf[9 + b] for b in range(3)]
    mix = [[sum(pf[3 * b + a] * ps[3 * b + c] for b in range(3)) for c in range(3)] for a in range(3)]
    base = [sum(pf[3 * b + a] * shift[b] for b in range(3)) for a in range(3)]
    alpha = [mix[a][0] * inv_f for a in range(3)]
    beta = [mix[a][1] * inv_f for a in range(3)]
    tile = (edges, LANES)
    wide_base = [jnp.broadcast_to(x, tile) for x in base]

    period = 3 * LANES
    lines = period // W
    lane = iota((1, LANES), 1)
    us = []
    vs = []
    for k in range(3):
        index = lane + k * LANES
        line = sum((index >= W * (j + 1)).astype(jnp.int32) for j in range(lines - 1))
        us.append((index - line * W).astype(f32) - (W - 1) / 2.0)
        vs.append(line.astype(f32) - (H - 1) / 2.0)
    start = [[alpha[a] * us[k] + (beta[a] * vs[k] + mix[a][2]) for a in range(3)] for k in range(3)]
    slope = [jnp.broadcast_to(beta[a] * float(lines), tile) for a in range(3)]

    def step(i, sums):
        s_acc, d_acc, e_acc = list(sums[:3]), list(sums[3:12]), list(sums[12:])
        rise = [slope[a] * float(i) for a in range(3)]
        for k in range(3):
            at = pl.ds(i * period + k * LANES, LANES)
            dep = depth_s[:, at]
            weight = conf[:, at].astype(f32)
            grad = None
            for a in range(3):
                q = start[k][a] + rise[a]
                r = weight * (dep * q + (wide_base[a] - points[a, :, at].astype(f32)))
                t = r * dep
                grad = t * q if grad is None else grad + t * q
                s_acc[a] = s_acc[a] + r
                d_acc[3 * k + a] = d_acc[3 * k + a] + t
            grad_s[:, at] = grad.astype(bf16)
        for a in range(3):
            e_acc[a] = e_acc[a] + ((d_acc[a] + d_acc[3 + a]) + d_acc[6 + a])
        return (*s_acc, *d_acc, *e_acc)

    steps = shards * pixels // period
    sums = (jnp.zeros(tile, f32),) * 15
    for s in range(shards):
        for i in range(steps // shards):
            sums = step(s * (steps // shards) + i, sums)
        placed = dot(sel, grad_s[:, s * pixels : (s + 1) * pixels], ((0,), (0,))).astype(bf16)
        out[s, :, :, :pixels] = placed.reshape(groups, cap, pixels)

    def total(x):
        return jnp.sum(x, axis=1, keepdims=True)

    d_acc = sums[3:12]
    d_all = [(d_acc[a] + d_acc[3 + a]) + d_acc[6 + a] for a in range(3)]
    s_sum = [total(x) for x in sums[:3]]
    d_sum = [total(x) for x in d_all]
    u_sum = [total(sum(d_acc[3 * k + a] * us[k] for k in range(3))) for a in range(3)]
    v_sum = [
        total(
            sum(d_acc[3 * k + a] * vs[k] for k in range(3))
            + float(lines) * (float(steps) * d_all[a] - sums[12 + a])
        )
        for a in range(3)
    ]

    moments = [[u_sum[a] * inv_f, v_sum[a] * inv_f, d_sum[a]] for a in range(3)]
    grad_first = [None] * 12
    grad_second = [None] * 13
    for b in range(3):
        for a in range(3):
            grad_first[3 * b + a] = sum(ps[3 * b + c] * moments[a][c] for c in range(3)) + shift[b] * s_sum[a]
        for c in range(3):
            grad_second[3 * b + c] = sum(pf[3 * b + a] * moments[a][c] for a in range(3))
        grad_second[9 + b] = sum(pf[3 * b + a] * s_sum[a] for a in range(3))
        grad_first[9 + b] = -grad_second[9 + b]
    grad_second[12] = -sum(alpha[a] * u_sum[a] + beta[a] * v_sum[a] for a in range(3))
    component = iota(tile, 1) // 8
    tables = []
    for grads in (grad_first, grad_second):
        table = jnp.zeros(tile, f32)
        for k, g in enumerate(grads):
            table = jnp.where(component == k, g, table)
        tables.append(table)
    table = jnp.where(lane_mask, jnp.concatenate(tables, axis=0), 0.0)
    lead = table.astype(bf16)
    rest = (table - lead.astype(f32)).astype(bf16)
    both_row = jnp.concatenate([mine_t[0:1, :], mine_t[1:2, :]], axis=1)
    owner_hot = hot(iota((slots, 2 * edges), 0) // cap == place(both_row))
    owned = dot(owner_hot, lead) + dot(owner_hot, rest)
    out[:, :, :, pixels:] = two_parts(owned).reshape(shards, groups, cap, LANES)


def call(kernel, outs, scratch=(), in_specs=None, mib=40):
    extra = {} if in_specs is None else {"in_specs": in_specs}
    return pl.pallas_call(
        kernel,
        out_shape=outs,
        scratch_shapes=list(scratch),
        compiler_params=pltpu.CompilerParams(vmem_limit_bytes=mib * 1024 * 1024),
        **extra,
    )


def shards(log_depth, depth_m, depth_v, pose, pose_m, pose_v, pairs, points, conf):
    n_view = lax.axis_size("view")
    n_edge = lax.axis_size("edge")
    owners = n_view * n_edge
    views, pixels = log_depth.shape
    edges = points.shape[0]
    width = pixels + LANES

    S = jax.ShapeDtypeStruct
    message = S((owners, CAP, width), bf16)
    depth_out = [S((views, pixels), f32)] * 3
    exchange = functools.partial(
        lax.all_to_all, axis_name=("edge", "view"), split_axis=0, concat_axis=0, tiled=True
    )

    poses = [pose.T, pose_m.T, pose_v.T]
    depths = [log_depth, depth_m, depth_v]
    hbm = pl.BlockSpec(memory_space=pltpu.HBM)
    sending, picker, mine, mine_t = call(
        first_kernel,
        [message, S((owners * CAP, views), bf16), S((edges, 2), jnp.int32), S((2, edges), jnp.int32)],
        [
            pltpu.VMEM((pairs.shape[0] // LANES, 2, LANES), jnp.int32),
            pltpu.VMEM((views, pixels), f32),
            pltpu.VMEM((8, ROWS), f32),
            pltpu.SemaphoreType.DMA((3,)),
        ],
        [hbm, hbm, hbm],
        40,
    )(*[pltpu.with_memory_space_constraint(x, pltpu.HBM) for x in (pairs.T.reshape(2, -1, LANES).transpose(1, 0, 2), log_depth, poses[0])])
    planes = points.transpose(1, 0, 2)
    for turn in range(ITERS):
        arrived = exchange(sending).reshape(n_edge, n_view, CAP, width)
        back = call(
            edge_kernel,
            S((n_edge, n_view, CAP, width), bf16),
            [
                pltpu.VMEM((edges, pixels * n_edge), f32),
                pltpu.VMEM((edges, pixels * n_edge), bf16),
            ],
        )(arrived, mine, mine_t, planes, conf)
        incoming = exchange(back.reshape(owners, CAP, width))
        last = turn == ITERS - 1
        kernel = functools.partial(owner_kernel, STEPS_DONE + turn + 1, last)
        pose_out = [S((8, ROWS) if last else (1, LANES), f32)] * 3
        results = call(kernel, depth_out + pose_out + ([] if last else [message]))(
            incoming, picker, *depths, *poses
        )
        depths, poses = results[:3], results[3:6]
        if not last:
            sending = results[6]
    return (*depths, *[p.T for p in poses])


def solution(mesh):
    depth = P("view", "edge")
    pose = P(None, ("view", "edge"))
    in_specs = (depth,) * 3 + (pose,) * 3 + (P(), P(("view", "edge"), None, None), P(("view", "edge"), None))
    out_specs = (depth,) * 3 + (pose,) * 3
    return jax.shard_map(shards, mesh=mesh, in_specs=in_specs, out_specs=out_specs, check_vma=False)
```

```python
import functools

import jax
import jax.numpy as jnp
from jax import lax
from jax.experimental import pallas as pl
from jax.experimental.pallas import tpu as pltpu
from jax.sharding import PartitionSpec as P

H = 128
W = 96
ITERS = 2
STEPS_DONE = 10
ROWS = 13
LANES = 128
CAP = 2
SHARDS = 8
SIDE = 4
ORDER = ("y", "z", "core", "x")

learn_rate = 0.01
beta_first = 0.9
beta_second = 0.999
adam_eps = 1e-08

f32 = jnp.float32
bf16 = jnp.bfloat16
EXACT = lax.Precision.HIGHEST


def adam(param, moment, second, half, count, scale):
    moment = beta_first * moment + ((1.0 - beta_first) * scale) * half
    second = beta_second * second + ((1.0 - beta_second) * scale * scale) * (half * half)
    corrected = moment * (learn_rate / (1.0 - beta_first**count))
    spread = second * (1.0 / (1.0 - beta_second**count))
    return (param - corrected / (jnp.sqrt(spread) + adam_eps), moment, second)


def iota(shape, dim):
    return lax.broadcasted_iota(jnp.int32, shape, dim)


def dot(a, b, dims=((1,), (0,)), precision=None):
    return lax.dot_general(a, b, (dims, ((), ())), precision=precision, preferred_element_type=f32)


def fold_matrix():
    return (iota((LANES, LANES), 0) // 8 == iota((LANES, LANES), 1)).astype(f32)


def hot(mask):
    return jnp.where(mask, 1.0, 0.0).astype(bf16)


def make_picker(seconds, start, views):
    lines = seconds.shape[0]
    slots = lines * 8 * CAP
    local = seconds - start
    value = jnp.where((local >= 0) & (local < views), local + 1, 0).astype(f32).astype(bf16)
    row = iota((slots, LANES), 0)
    lane = iota((slots, LANES), 1)
    place = row // CAP
    block = place % SIDE * SIDE + place // (SIDE * SHARDS)
    spread = dot(hot(block[:, :lines] == lane[:, :lines]), value)
    hit = (spread > 0.5) & (lane // 16 == place // SIDE % SHARDS)
    tri = hot(iota((LANES, LANES), 0) < iota((LANES, LANES), 1))
    rank = dot(hot(hit), tri)
    mine = hit & (rank == (row % CAP).astype(f32))
    target = jnp.sum(jnp.where(mine, spread, 0.0), axis=1, keepdims=True)
    return hot((iota((slots, views), 1) + 1).astype(f32) == target)


def spread_pose(pose_t):
    lane = iota((8, LANES), 1)
    wide = jnp.zeros((8, LANES), f32)
    for k in range(ROWS):
        wide = jnp.where(lane == iota((8, LANES), 0) + 8 * k, pose_t[:, k : k + 1], wide)
    return jnp.sum(wide, axis=0, keepdims=True)


def gather_pose(row):
    wide = jnp.broadcast_to(row, (8, LANES))
    mine = iota(wide.shape, 1) % 8 == iota(wide.shape, 0)
    return dot(jnp.where(mine, wide, 0.0), fold_matrix()[:, :ROWS], ((1,), (0,)), EXACT)


def two_parts(rows):
    lead = rows.astype(bf16).astype(f32)
    even = iota(rows.shape, 0) % 2 == 0
    return jnp.where(even, lead, rows - lead).astype(bf16)


def send_rows(out, picker, depth, pose_row):
    owners, cap, width = out.shape
    pixels = width - LANES
    picked = dot(picker, depth.astype(bf16)).astype(bf16)
    out[:, :, :pixels] = picked.reshape(owners, cap, pixels)
    wide = jnp.broadcast_to(pose_row, (owners * cap, LANES))
    out[:, :, pixels:] = two_parts(wide).reshape(owners, cap, LANES)


def first_kernel(pairs_hbm, depth_hbm, pose_hbm, out, picker_out, mine, mine_t, pairs, depth, pose_t, sems):
    sources = (pairs_hbm, pose_hbm, depth_hbm)
    copies = [
        pltpu.make_async_copy(src, dst, sems.at[k])
        for k, (src, dst) in enumerate(zip(sources, (pairs, pose_t, depth)))
    ]
    for copy in copies:
        copy.start()
    copies[0].wait()
    views = depth.shape[0]
    picker = make_picker(pairs[:, 1, :], lax.axis_index(("x", "y")) * views, views)
    picker_out[...] = picker
    copies[1].wait()
    row = spread_pose(pose_t[...])
    copies[2].wait()
    send_rows(out, picker, depth[...], row)

    edges = mine.shape[0]
    me = lax.axis_index(("x", "y")) * SHARDS + lax.axis_index(("z", "core"))
    line = pairs[me // (LANES // edges)].astype(f32)
    lanes = iota((edges, LANES), 1)
    pick = (lanes == me % (LANES // edges) * edges + iota((edges, LANES), 0)).astype(f32)
    for ref, value in (
        (mine, dot(pick, line, ((1,), (1,)), EXACT)),
        (mine_t, dot(line, pick, ((1,), (1,)), EXACT)),
    ):
        ref[...] = (value + 0.5).astype(jnp.int32)


def owner_kernel(count, last, incoming, picker, depth, m, v, pose_t, pose_m, pose_v, *outs):
    owners, cap, width = incoming.shape
    pixels = width - LANES
    grad = dot(picker[...], incoming[:, :, :pixels].reshape(owners * cap, pixels), ((0,), (0,)))
    new = adam(depth[...], m[...], v[...], grad, count, 2.0)
    for ref, value in zip(outs[:3], new):
        ref[...] = value
    rows = incoming[:, :, pixels:].reshape(owners * cap, LANES)
    pose_grad = jnp.sum(rows.astype(f32), axis=0, keepdims=True)
    state = [ref[...] if last else spread_pose(ref[...]) for ref in (pose_t, pose_m, pose_v)]
    new_pose = adam(*state, pose_grad, count, 2.0 / (H * W))
    for ref, value in zip(outs[3:6], new_pose):
        ref[...] = gather_pose(value) if last else value
    if not last:
        send_rows(outs[6], picker[...], new[0], new_pose[0])


def edge_kernel(arrived, mine, mine_t, points, conf, out, depth_s, grad_s):
    side_y, shards, side_x, cap, width = arrived.shape
    groups = side_y * side_x
    pixels = width - LANES
    edges = mine.shape[0]
    slots = shards * groups * cap

    def place(view):
        block = view // (8 * shards)
        return (block % side_y * shards + view // 8 % shards) * side_x + block // side_y

    both = jnp.concatenate([mine[:, 0:1], mine[:, 1:2]], axis=0)
    pose_rows = arrived[:, :, :, :, pixels:].reshape(slots, LANES)
    slot_of = iota((2 * edges, slots), 1)
    lane_mask = iota((2 * edges, LANES), 1) % 8 == both % 8
    fold = hot(iota((LANES, LANES), 0) // 8 == iota((LANES, LANES), 1))
    poses = None
    for part in range(cap):
        picked = dot(hot(slot_of == place(both) * cap + part), pose_rows)
        part_poses = dot(jnp.where(lane_mask, picked, 0.0).astype(bf16), fold)
        poses = part_poses if poses is None else poses + part_poses

    group = mine[:, 1:2] // 64
    line = group % side_y * side_x + group // side_y
    group_row = mine_t[1:2, :] // 64
    earlier = iota((edges, edges), 1) < iota((edges, edges), 0)
    slot = jnp.sum(jnp.where((group == group_row) & earlier, 1.0, 0.0), axis=1, keepdims=True)
    sel = hot((line * cap).astype(f32) + slot == iota((edges, groups * cap), 1).astype(f32))
    for s in range(shards):
        rows = arrived[:, s, :, :, :pixels].reshape(groups * cap, pixels)
        depth_s[:, s * pixels : (s + 1) * pixels] = jnp.exp(dot(sel, rows))

    pf = [poses[:edges, k : k + 1] for k in range(12)]
    ps = [poses[edges:, k : k + 1] for k in range(13)]
    inv_f = jnp.exp(-ps[12])
    shift = [ps[9 + b] - pf[9 + b] for b in range(3)]
    mix = [[sum(pf[3 * b + a] * ps[3 * b + c] for b in range(3)) for c in range(3)] for a in range(3)]
    base = [sum(pf[3 * b + a] * shift[b] for b in range(3)) for a in range(3)]
    alpha = [mix[a][0] * inv_f for a in range(3)]
    beta = [mix[a][1] * inv_f for a in range(3)]
    tile = (edges, LANES)
    wide_base = [jnp.broadcast_to(x, tile) for x in base]

    period = 3 * LANES
    lines = period // W
    lane = iota((1, LANES), 1)
    us = []
    vs = []
    for k in range(3):
        index = lane + k * LANES
        line = sum((index >= W * (j + 1)).astype(jnp.int32) for j in range(lines - 1))
        us.append((index - line * W).astype(f32) - (W - 1) / 2.0)
        vs.append(line.astype(f32) - (H - 1) / 2.0)
    start = [[alpha[a] * us[k] + (beta[a] * vs[k] + mix[a][2]) for a in range(3)] for k in range(3)]
    slope = [jnp.broadcast_to(beta[a] * float(lines), tile) for a in range(3)]

    def step(i, sums):
        s_acc, d_acc, e_acc = list(sums[:3]), list(sums[3:12]), list(sums[12:])
        rise = [slope[a] * float(i) for a in range(3)]
        for k in range(3):
            at = pl.ds(i * period + k * LANES, LANES)
            dep = depth_s[:, at]
            weight = conf[:, at].astype(f32)
            grad = None
            for a in range(3):
                q = start[k][a] + rise[a]
                r = weight * (dep * q + (wide_base[a] - points[a, :, at].astype(f32)))
                t = r * dep
                grad = t * q if grad is None else grad + t * q
                s_acc[a] = s_acc[a] + r
                d_acc[3 * k + a] = d_acc[3 * k + a] + t
            grad_s[:, at] = grad.astype(bf16)
        for a in range(3):
            e_acc[a] = e_acc[a] + ((d_acc[a] + d_acc[3 + a]) + d_acc[6 + a])
        return (*s_acc, *d_acc, *e_acc)

    steps = shards * pixels // period
    sums = (jnp.zeros(tile, f32),) * 15
    for s in range(shards):
        for i in range(steps // shards):
            sums = step(s * (steps // shards) + i, sums)
        placed = dot(sel, grad_s[:, s * pixels : (s + 1) * pixels], ((0,), (0,))).astype(bf16)
        out[:, s, :, :, :pixels] = placed.reshape(side_y, side_x, cap, pixels)

    def total(x):
        return jnp.sum(x, axis=1, keepdims=True)

    d_acc = sums[3:12]
    d_all = [(d_acc[a] + d_acc[3 + a]) + d_acc[6 + a] for a in range(3)]
    s_sum = [total(x) for x in sums[:3]]
    d_sum = [total(x) for x in d_all]
    u_sum = [total(sum(d_acc[3 * k + a] * us[k] for k in range(3))) for a in range(3)]
    v_sum = [
        total(
            sum(d_acc[3 * k + a] * vs[k] for k in range(3))
            + float(lines) * (float(steps) * d_all[a] - sums[12 + a])
        )
        for a in range(3)
    ]

    moments = [[u_sum[a] * inv_f, v_sum[a] * inv_f, d_sum[a]] for a in range(3)]
    grad_first = [None] * 12
    grad_second = [None] * 13
    for b in range(3):
        for a in range(3):
            grad_first[3 * b + a] = sum(ps[3 * b + c] * moments[a][c] for c in range(3)) + shift[b] * s_sum[a]
        for c in range(3):
            grad_second[3 * b + c] = sum(pf[3 * b + a] * moments[a][c] for a in range(3))
        grad_second[9 + b] = sum(pf[3 * b + a] * s_sum[a] for a in range(3))
        grad_first[9 + b] = -grad_second[9 + b]
    grad_second[12] = -sum(alpha[a] * u_sum[a] + beta[a] * v_sum[a] for a in range(3))
    component = iota(tile, 1) // 8
    tables = []
    for grads in (grad_first, grad_second):
        table = jnp.zeros(tile, f32)
        for k, g in enumerate(grads):
            table = jnp.where(component == k, g, table)
        tables.append(table)
    table = jnp.where(lane_mask, jnp.concatenate(tables, axis=0), 0.0)
    lead = table.astype(bf16)
    rest = (table - lead.astype(f32)).astype(bf16)
    both_row = jnp.concatenate([mine_t[0:1, :], mine_t[1:2, :]], axis=1)
    owner_hot = hot(iota((slots, 2 * edges), 0) // cap == place(both_row))
    owned = dot(owner_hot, lead) + dot(owner_hot, rest)
    out[:, :, :, :, pixels:] = two_parts(owned).reshape(side_y, shards, side_x, cap, LANES)


def call(kernel, outs, scratch=(), in_specs=None, mib=40):
    extra = {} if in_specs is None else {"in_specs": in_specs}
    return pl.pallas_call(
        kernel,
        out_shape=outs,
        scratch_shapes=list(scratch),
        compiler_params=pltpu.CompilerParams(vmem_limit_bytes=mib * 1024 * 1024),
        **extra,
    )


def shards(log_depth, depth_m, depth_v, pose, pose_m, pose_v, pairs, points, conf):
    n_view = lax.axis_size("x") * lax.axis_size("y")
    n_edge = lax.axis_size("z") * lax.axis_size("core")
    owners = n_view * n_edge
    views, pixels = log_depth.shape
    edges = points.shape[0]
    width = pixels + LANES

    S = jax.ShapeDtypeStruct
    message = S((owners, CAP, width), bf16)
    depth_out = [S((views, pixels), f32)] * 3
    exchange = functools.partial(
        lax.all_to_all, axis_name=ORDER, split_axis=0, concat_axis=0, tiled=True
    )

    poses = [pose.T, pose_m.T, pose_v.T]
    depths = [log_depth, depth_m, depth_v]
    hbm = pl.BlockSpec(memory_space=pltpu.HBM)
    sending, picker, mine, mine_t = call(
        first_kernel,
        [message, S((owners * CAP, views), bf16), S((edges, 2), jnp.int32), S((2, edges), jnp.int32)],
        [
            pltpu.VMEM((pairs.shape[0] // LANES, 2, LANES), jnp.int32),
            pltpu.VMEM((views, pixels), f32),
            pltpu.VMEM((8, ROWS), f32),
            pltpu.SemaphoreType.DMA((3,)),
        ],
        [hbm, hbm, hbm],
        40,
    )(*[pltpu.with_memory_space_constraint(x, pltpu.HBM) for x in (pairs.T.reshape(2, -1, LANES).transpose(1, 0, 2), log_depth, poses[0])])
    planes = points.transpose(1, 0, 2)
    for turn in range(ITERS):
        arrived = exchange(sending).reshape(SIDE, n_edge, SIDE, CAP, width)
        back = call(
            edge_kernel,
            S((SIDE, n_edge, SIDE, CAP, width), bf16),
            [
                pltpu.VMEM((edges, pixels * n_edge), f32),
                pltpu.VMEM((edges, pixels * n_edge), bf16),
            ],
        )(arrived, mine, mine_t, planes, conf)
        incoming = exchange(back.reshape(owners, CAP, width))
        last = turn == ITERS - 1
        kernel = functools.partial(owner_kernel, STEPS_DONE + turn + 1, last)
        pose_out = [S((8, ROWS) if last else (1, LANES), f32)] * 3
        results = call(kernel, depth_out + pose_out + ([] if last else [message]))(
            incoming, picker, *depths, *poses
        )
        depths, poses = results[:3], results[3:6]
        if not last:
            sending = results[6]
    return (*depths, *[p.T for p in poses])


def solution(mesh):
    grid = jax.sharding.Mesh(mesh.devices.reshape(SIDE, SIDE, SIDE, -1), ("x", "y", "z", "core"))
    view, edge = ("x", "y"), ("z", "core")
    depth = P(view, edge)
    pose = P(None, view + edge)
    in_specs = (depth,) * 3 + (pose,) * 3 + (P(), P(view + edge, None, None), P(view + edge, None))
    out_specs = (depth,) * 3 + (pose,) * 3
    return jax.shard_map(shards, mesh=grid, in_specs=in_specs, out_specs=out_specs, check_vma=False)
```

```python
import functools

import jax
import jax.numpy as jnp
from jax import lax
from jax.experimental import pallas as pl
from jax.experimental.pallas import tpu as pltpu
from jax.sharding import PartitionSpec as P

H = 128
W = 96
ITERS = 2
STEPS_DONE = 10
ROWS = 13
LANES = 128
CAP = 2
CORES = 2
SIDE = 4
SHARDS = SIDE * CORES
ORDER = ("core", "x", "y", "z")

learn_rate = 0.01
beta_first = 0.9
beta_second = 0.999
adam_eps = 1e-08

f32 = jnp.float32
bf16 = jnp.bfloat16
EXACT = lax.Precision.HIGHEST


def adam(param, moment, second, half, count, scale):
    moment = beta_first * moment + ((1.0 - beta_first) * scale) * half
    second = beta_second * second + ((1.0 - beta_second) * scale * scale) * (half * half)
    corrected = moment * (learn_rate / (1.0 - beta_first**count))
    spread = second * (1.0 / (1.0 - beta_second**count))
    return (param - corrected / (jnp.sqrt(spread) + adam_eps), moment, second)


def iota(shape, dim):
    return lax.broadcasted_iota(jnp.int32, shape, dim)


def dot(a, b, dims=((1,), (0,)), precision=None):
    return lax.dot_general(a, b, (dims, ((), ())), precision=precision, preferred_element_type=f32)


def fold_matrix():
    return (iota((LANES, LANES), 0) // 8 == iota((LANES, LANES), 1)).astype(f32)


def hot(mask):
    return jnp.where(mask, 1.0, 0.0).astype(bf16)


def make_picker(seconds, start, views):
    lines = seconds.shape[0]
    slots = lines * 8 * CAP
    local = seconds - start
    value = jnp.where((local >= 0) & (local < views), local + 1, 0).astype(f32).astype(bf16)
    row = iota((slots, LANES), 0)
    lane = iota((slots, LANES), 1)
    place = row // CAP
    spread = dot(hot(place[:, :lines] // SIDE % lines == lane[:, :lines]), value)
    hit = (spread > 0.5) & (lane // 16 == place % SIDE * CORES + place // (lines * SIDE))
    tri = hot(iota((LANES, LANES), 0) < iota((LANES, LANES), 1))
    rank = dot(hot(hit), tri)
    mine = hit & (rank == (row % CAP).astype(f32))
    target = jnp.sum(jnp.where(mine, spread, 0.0), axis=1, keepdims=True)
    return hot((iota((slots, views), 1) + 1).astype(f32) == target)


def spread_pose(pose_t):
    lane = iota((8, LANES), 1)
    wide = jnp.zeros((8, LANES), f32)
    for k in range(ROWS):
        wide = jnp.where(lane == iota((8, LANES), 0) + 8 * k, pose_t[:, k : k + 1], wide)
    return jnp.sum(wide, axis=0, keepdims=True)


def gather_pose(row):
    wide = jnp.broadcast_to(row, (8, LANES))
    mine = iota(wide.shape, 1) % 8 == iota(wide.shape, 0)
    return dot(jnp.where(mine, wide, 0.0), fold_matrix()[:, :ROWS], ((1,), (0,)), EXACT)


def two_parts(rows):
    lead = rows.astype(bf16).astype(f32)
    even = iota(rows.shape, 0) % 2 == 0
    return jnp.where(even, lead, rows - lead).astype(bf16)


def send_rows(out, picker, depth, pose_row):
    owners, cap, width = out.shape
    pixels = width - LANES
    picked = dot(picker, depth.astype(bf16)).astype(bf16)
    out[:, :, :pixels] = picked.reshape(owners, cap, pixels)
    wide = jnp.broadcast_to(pose_row, (owners * cap, LANES))
    out[:, :, pixels:] = two_parts(wide).reshape(owners, cap, LANES)


def first_kernel(pairs_hbm, depth_hbm, pose_hbm, out, picker_out, mine, mine_t, pairs, depth, pose_t, sems):
    sources = (pairs_hbm, pose_hbm, depth_hbm)
    copies = [
        pltpu.make_async_copy(src, dst, sems.at[k])
        for k, (src, dst) in enumerate(zip(sources, (pairs, pose_t, depth)))
    ]
    for copy in copies:
        copy.start()
    copies[0].wait()
    views = depth.shape[0]
    picker = make_picker(pairs[:, 1, :], lax.axis_index(("x", "y")) * views, views)
    picker_out[...] = picker
    copies[1].wait()
    row = spread_pose(pose_t[...])
    copies[2].wait()
    send_rows(out, picker, depth[...], row)

    edges = mine.shape[0]
    me = lax.axis_index(("x", "y")) * SHARDS + lax.axis_index(("z", "core"))
    line = pairs[me // (LANES // edges)].astype(f32)
    lanes = iota((edges, LANES), 1)
    pick = (lanes == me % (LANES // edges) * edges + iota((edges, LANES), 0)).astype(f32)
    for ref, value in (
        (mine, dot(pick, line, ((1,), (1,)), EXACT)),
        (mine_t, dot(line, pick, ((1,), (1,)), EXACT)),
    ):
        ref[...] = (value + 0.5).astype(jnp.int32)


def owner_kernel(count, last, incoming, picker, depth, m, v, pose_t, pose_m, pose_v, *outs):
    owners, cap, width = incoming.shape
    pixels = width - LANES
    grad = dot(picker[...], incoming[:, :, :pixels].reshape(owners * cap, pixels), ((0,), (0,)))
    new = adam(depth[...], m[...], v[...], grad, count, 2.0)
    for ref, value in zip(outs[:3], new):
        ref[...] = value
    rows = incoming[:, :, pixels:].reshape(owners * cap, LANES)
    pose_grad = jnp.sum(rows.astype(f32), axis=0, keepdims=True)
    state = [ref[...] if last else spread_pose(ref[...]) for ref in (pose_t, pose_m, pose_v)]
    new_pose = adam(*state, pose_grad, count, 2.0 / (H * W))
    for ref, value in zip(outs[3:6], new_pose):
        ref[...] = gather_pose(value) if last else value
    if not last:
        send_rows(outs[6], picker[...], new[0], new_pose[0])


def edge_kernel(arrived, mine, mine_t, points, conf, out, depth_s, grad_s):
    cores, groups, side, cap, width = arrived.shape
    shards = cores * side
    pixels = width - LANES
    edges = mine.shape[0]
    slots = shards * groups * cap

    def place(view):
        shard = view // 8 % shards
        return (shard % cores * groups + view // (8 * shards)) * side + shard // cores

    both = jnp.concatenate([mine[:, 0:1], mine[:, 1:2]], axis=0)
    pose_rows = arrived[:, :, :, :, pixels:].reshape(slots, LANES)
    slot_of = iota((2 * edges, slots), 1)
    lane_mask = iota((2 * edges, LANES), 1) % 8 == both % 8
    fold = hot(iota((LANES, LANES), 0) // 8 == iota((LANES, LANES), 1))
    poses = None
    for part in range(cap):
        picked = dot(hot(slot_of == place(both) * cap + part), pose_rows)
        part_poses = dot(jnp.where(lane_mask, picked, 0.0).astype(bf16), fold)
        poses = part_poses if poses is None else poses + part_poses

    group = mine[:, 1:2] // 64
    group_row = mine_t[1:2, :] // 64
    earlier = iota((edges, edges), 1) < iota((edges, edges), 0)
    slot = jnp.sum(jnp.where((group == group_row) & earlier, 1.0, 0.0), axis=1, keepdims=True)
    sel = hot((group * cap).astype(f32) + slot == iota((edges, groups * cap), 1).astype(f32))
    for s in range(shards):
        rows = arrived[s % cores, :, s // cores, :, :pixels].reshape(groups * cap, pixels)
        depth_s[:, s * pixels : (s + 1) * pixels] = jnp.exp(dot(sel, rows))

    pf = [poses[:edges, k : k + 1] for k in range(12)]
    ps = [poses[edges:, k : k + 1] for k in range(13)]
    inv_f = jnp.exp(-ps[12])
    shift = [ps[9 + b] - pf[9 + b] for b in range(3)]
    mix = [[sum(pf[3 * b + a] * ps[3 * b + c] for b in range(3)) for c in range(3)] for a in range(3)]
    base = [sum(pf[3 * b + a] * shift[b] for b in range(3)) for a in range(3)]
    alpha = [mix[a][0] * inv_f for a in range(3)]
    beta = [mix[a][1] * inv_f for a in range(3)]
    tile = (edges, LANES)
    wide_base = [jnp.broadcast_to(x, tile) for x in base]

    period = 3 * LANES
    lines = period // W
    lane = iota((1, LANES), 1)
    us = []
    vs = []
    for k in range(3):
        index = lane + k * LANES
        line = sum((index >= W * (j + 1)).astype(jnp.int32) for j in range(lines - 1))
        us.append((index - line * W).astype(f32) - (W - 1) / 2.0)
        vs.append(line.astype(f32) - (H - 1) / 2.0)
    start = [[alpha[a] * us[k] + (beta[a] * vs[k] + mix[a][2]) for a in range(3)] for k in range(3)]
    slope = [jnp.broadcast_to(beta[a] * float(lines), tile) for a in range(3)]

    def step(i, sums):
        s_acc, d_acc, e_acc = list(sums[:3]), list(sums[3:12]), list(sums[12:])
        rise = [slope[a] * float(i) for a in range(3)]
        for k in range(3):
            at = pl.ds(i * period + k * LANES, LANES)
            dep = depth_s[:, at]
            weight = conf[:, at].astype(f32)
            grad = None
            for a in range(3):
                q = start[k][a] + rise[a]
                r = weight * (dep * q + (wide_base[a] - points[a, :, at].astype(f32)))
                t = r * dep
                grad = t * q if grad is None else grad + t * q
                s_acc[a] = s_acc[a] + r
                d_acc[3 * k + a] = d_acc[3 * k + a] + t
            grad_s[:, at] = grad.astype(bf16)
        for a in range(3):
            e_acc[a] = e_acc[a] + ((d_acc[a] + d_acc[3 + a]) + d_acc[6 + a])
        return (*s_acc, *d_acc, *e_acc)

    steps = shards * pixels // period
    sums = (jnp.zeros(tile, f32),) * 15
    for s in range(shards):
        for i in range(steps // shards):
            sums = step(s * (steps // shards) + i, sums)
        placed = dot(sel, grad_s[:, s * pixels : (s + 1) * pixels], ((0,), (0,))).astype(bf16)
        out[s % cores, :, s // cores, :, :pixels] = placed.reshape(groups, cap, pixels)

    def total(x):
        return jnp.sum(x, axis=1, keepdims=True)

    d_acc = sums[3:12]
    d_all = [(d_acc[a] + d_acc[3 + a]) + d_acc[6 + a] for a in range(3)]
    s_sum = [total(x) for x in sums[:3]]
    d_sum = [total(x) for x in d_all]
    u_sum = [total(sum(d_acc[3 * k + a] * us[k] for k in range(3))) for a in range(3)]
    v_sum = [
        total(
            sum(d_acc[3 * k + a] * vs[k] for k in range(3))
            + float(lines) * (float(steps) * d_all[a] - sums[12 + a])
        )
        for a in range(3)
    ]

    moments = [[u_sum[a] * inv_f, v_sum[a] * inv_f, d_sum[a]] for a in range(3)]
    grad_first = [None] * 12
    grad_second = [None] * 13
    for b in range(3):
        for a in range(3):
            grad_first[3 * b + a] = sum(ps[3 * b + c] * moments[a][c] for c in range(3)) + shift[b] * s_sum[a]
        for c in range(3):
            grad_second[3 * b + c] = sum(pf[3 * b + a] * moments[a][c] for a in range(3))
        grad_second[9 + b] = sum(pf[3 * b + a] * s_sum[a] for a in range(3))
        grad_first[9 + b] = -grad_second[9 + b]
    grad_second[12] = -sum(alpha[a] * u_sum[a] + beta[a] * v_sum[a] for a in range(3))
    component = iota(tile, 1) // 8
    tables = []
    for grads in (grad_first, grad_second):
        table = jnp.zeros(tile, f32)
        for k, g in enumerate(grads):
            table = jnp.where(component == k, g, table)
        tables.append(table)
    table = jnp.where(lane_mask, jnp.concatenate(tables, axis=0), 0.0)
    lead = table.astype(bf16)
    rest = (table - lead.astype(f32)).astype(bf16)
    both_row = jnp.concatenate([mine_t[0:1, :], mine_t[1:2, :]], axis=1)
    owner_hot = hot(iota((slots, 2 * edges), 0) // cap == place(both_row))
    owned = dot(owner_hot, lead) + dot(owner_hot, rest)
    out[:, :, :, :, pixels:] = two_parts(owned).reshape(cores, groups, side, cap, LANES)


def call(kernel, outs, scratch=(), in_specs=None, mib=40):
    extra = {} if in_specs is None else {"in_specs": in_specs}
    return pl.pallas_call(
        kernel,
        out_shape=outs,
        scratch_shapes=list(scratch),
        compiler_params=pltpu.CompilerParams(vmem_limit_bytes=mib * 1024 * 1024),
        **extra,
    )


def shards(log_depth, depth_m, depth_v, pose, pose_m, pose_v, pairs, points, conf):
    n_view = lax.axis_size("x") * lax.axis_size("y")
    n_edge = lax.axis_size("z") * lax.axis_size("core")
    owners = n_view * n_edge
    views, pixels = log_depth.shape
    edges = points.shape[0]
    width = pixels + LANES

    S = jax.ShapeDtypeStruct
    message = S((owners, CAP, width), bf16)
    depth_out = [S((views, pixels), f32)] * 3
    exchange = functools.partial(
        lax.all_to_all, axis_name=ORDER, split_axis=0, concat_axis=0, tiled=True
    )

    poses = [pose.T, pose_m.T, pose_v.T]
    depths = [log_depth, depth_m, depth_v]
    hbm = pl.BlockSpec(memory_space=pltpu.HBM)
    sending, picker, mine, mine_t = call(
        first_kernel,
        [message, S((owners * CAP, views), bf16), S((edges, 2), jnp.int32), S((2, edges), jnp.int32)],
        [
            pltpu.VMEM((pairs.shape[0] // LANES, 2, LANES), jnp.int32),
            pltpu.VMEM((views, pixels), f32),
            pltpu.VMEM((8, ROWS), f32),
            pltpu.SemaphoreType.DMA((3,)),
        ],
        [hbm, hbm, hbm],
        40,
    )(*[pltpu.with_memory_space_constraint(x, pltpu.HBM) for x in (pairs.T.reshape(2, -1, LANES).transpose(1, 0, 2), log_depth, poses[0])])
    planes = points.transpose(1, 0, 2)
    for turn in range(ITERS):
        arrived = exchange(sending).reshape(CORES, n_view, SIDE, CAP, width)
        back = call(
            edge_kernel,
            S((CORES, n_view, SIDE, CAP, width), bf16),
            [
                pltpu.VMEM((edges, pixels * n_edge), f32),
                pltpu.VMEM((edges, pixels * n_edge), bf16),
            ],
        )(arrived, mine, mine_t, planes, conf)
        incoming = exchange(back.reshape(owners, CAP, width))
        last = turn == ITERS - 1
        kernel = functools.partial(owner_kernel, STEPS_DONE + turn + 1, last)
        pose_out = [S((8, ROWS) if last else (1, LANES), f32)] * 3
        results = call(kernel, depth_out + pose_out + ([] if last else [message]))(
            incoming, picker, *depths, *poses
        )
        depths, poses = results[:3], results[3:6]
        if not last:
            sending = results[6]
    return (*depths, *[p.T for p in poses])


def solution(mesh):
    grid = jax.sharding.Mesh(mesh.devices.reshape(SIDE, SIDE, SIDE, CORES), ("x", "y", "z", "core"))
    view, edge = ("x", "y"), ("z", "core")
    depth = P(view, edge)
    pose = P(None, view + edge)
    in_specs = (depth,) * 3 + (pose,) * 3 + (P(), P(view + edge, None, None), P(view + edge, None))
    out_specs = (depth,) * 3 + (pose,) * 3
    return jax.shard_map(shards, mesh=grid, in_specs=in_specs, out_specs=out_specs, check_vma=False)
```
